32 devices in a mesh: grp: 2 (over y), comp: 4 (over z), space: 4 (over x, core).
Axes of the slice: x: 2, y: 2, z: 4, core: 2. Of those that a mesh axis runs over, the one named last changes fastest.
Arguments:
- spectrum: float32 [2304, 4096], P('comp', ('grp', 'space')), parts along dimension 1, may hold values from -6 to 6
- wave_speed: float32 [36], replicated, may hold values from 0.25 to 2
- current_east: float32 [4096], P(('grp', 'space')), parts along dimension 0, may hold values from -3 to 3
- current_north: float32 [4096], P(('grp', 'space')), parts along dimension 0, may hold values from -3 to 3
- substeps: int32 [2304], replicated, may hold values from 1 to 4, as said below
- neighbours: int32 [4, 4096], P(None, ('grp', 'space')), parts along dimension 1, may hold values from 0 to 767, as said below
- blocks: bfloat16 [64, 64, 64], replicated, may hold values from -0.75 to 0.75
- quad_index: int32 [4, 64], replicated, may hold values from 0 to 35
- strength: float32 [64], replicated, may hold values from -1 to 1
Outputs:
- spectrum_out: float32 [2304, 4096], P('comp', ('grp', 'space')), parts along dimension 1
The draws below stay inside these ranges and needn't reach their ends.
There are 2 independent parts, one for each index of `grp`. The reference program is written for one: setup_inputs(seed, part) draws one part's arguments, and reference() takes and returns one part's arrays. A program takes and returns all parts, laid end to end along the dimension named above; an argument that names none is the same for every part. Nothing has to cross between parts.
Inputs may be any that keep to these rules, and one draw needn't show every extreme that they name: `substeps`: component 0 takes 4. `neighbours`: the entry of row r for the slab's point q (counted within its slab) is q + 128 + o, with -128 <= o <= -1 for rows 0 and 2 and 1 <= o <= 128 for rows 1 and 3.
All inputs are finite; a program needn't handle non-finite values.
Results may differ from the reference program's by a relative error of at most 0.00031.
Values sent between devices are 32-bit elements; how exact they have to be, the bound alone decides.
No kernel may reach another device: no remote copies, remote signals or barrier semaphores. Data moves between devices by JAX's collectives and lax.ppermute only.
A program may use at most 64 MiB of HBM per device.

```python
import math
import jax
import jax.numpy as jnp
from jax import lax

NF = 36
ND = 64
NBLK = 64
SUB = 4
HALO = 128
STEPS = 1
K = 2304
PTS_SLAB = 512
PTS = 2048


def draw_substeps(key, part):
    components = jnp.arange(NF * ND, dtype=jnp.int32)
    frequency = components // ND
    jitter = jax.random.randint(key, (NF * ND,), -1, 1, dtype=jnp.int32)
    counts = SUB - frequency * SUB // NF + jitter
    counts = jnp.clip(counts, 1, SUB)
    return counts.at[0].set(SUB).astype(jnp.int32)


def draw_neighbours(key, part):
    offsets = jax.random.randint(key, (4, PTS), 1, HALO + 1, dtype=jnp.int32)
    direction_sign = jnp.array([-1, 1, -1, 1], dtype=jnp.int32)[:, None]
    position = (jnp.arange(PTS, dtype=jnp.int32) % PTS_SLAB)[None, :]
    row_number = jnp.arange(4, dtype=jnp.int32)[:, None]
    extended = position + HALO + direction_sign * offsets
    extended = jnp.where((row_number == 0) & (position == 0), 0, extended)
    extended = jnp.where((row_number == 1) & (position == PTS_SLAB - 1), PTS_SLAB + 2 * HALO - 1, extended)
    return extended.astype(jnp.int32)


def draw_quad_index(key, part):
    table = jax.random.randint(key, (4, NBLK), 0, NF, dtype=jnp.int32)
    table = table.at[:, 0].set(0)
    table = table.at[:, 1].set(NF - 1)
    return table.astype(jnp.int32)


def shard_levels(own_key, extent, shards, least, high):
    level, own = 1.0, jax.random.fold_in(own_key, 6)
    for dim, shards_of in shards:
        steps = jnp.exp(jax.random.uniform(jax.random.fold_in(own, dim), (shards_of,), jnp.float32, least / len(shards), high / len(shards)))
        level = level * jnp.repeat(steps, extent[dim] // shards_of).reshape([-1 if axis == dim else 1 for axis in range(len(extent))])
    return level


def scatter_about(rng, extent, deviation, bound, cuts=(), held_as=jnp.bfloat16):
    result = deviation * jax.random.normal(rng, extent, jnp.float32)
    if cuts:
        result = result * shard_levels(rng, extent, cuts, -0.22, 0.18)
    return jnp.clip(result, -bound, bound).astype(held_as)


def setup_inputs(seed: int = 0, part: int = 0) -> dict:
    key_of = jax.random.split(jax.random.key(seed), 10)
    part_splits = jax.random.split(jax.random.fold_in(key_of[9], part), 10)
    return {
        "spectrum": scatter_about(part_splits[0], (K, PTS), 1.0, 6.0, ((0, 4), (1, 4)), jnp.float32),
        "wave_speed": jnp.clip(jnp.exp(jax.random.uniform(key_of[1], (NF,), jnp.float32, math.log(0.25), math.log(2.0))), 0.25, 2.0),
        "current_east": scatter_about(part_splits[2], (PTS,), 0.5, 3.0, ((0, 4),), jnp.float32),
        "current_north": scatter_about(part_splits[3], (PTS,), 0.5, 3.0, ((0, 4),), jnp.float32),
        "substeps": draw_substeps(jax.random.fold_in(key_of[9], 71), part),
        "neighbours": draw_neighbours(jax.random.fold_in(jax.random.fold_in(key_of[9], part), 71), part),
        "blocks": scatter_about(key_of[6], (NBLK, ND, ND), ND ** -0.5, 0.75),
        "quad_index": draw_quad_index(jax.random.fold_in(key_of[9], 71), part),
        "strength": jnp.clip(jax.random.uniform(key_of[8], (NBLK,), jnp.float32, -1.0, 1.0), -1.0, 1.0),
    }


courant_scale = 0.4
courant_limit = 0.45
source_step = 0.1


def reference(spectrum, wave_speed, current_east, current_north, substeps, neighbours, blocks, quad_index, strength):
    global_index = (jnp.arange(PTS, dtype=jnp.int32) // PTS_SLAB) * PTS_SLAB + neighbours
    angles = (jnp.arange(ND, dtype=jnp.float32) + 0.5) * (2.0 * math.pi / ND)

    def per_frequency(members):
        values, speed_value, counts = members
        divisor = counts.astype(jnp.float32)[:, None]
        along_x = jnp.clip(((speed_value * jnp.cos(angles))[:, None] + current_east[None, :]) * courant_scale / divisor, -courant_limit, courant_limit)
        along_y = jnp.clip(((speed_value * jnp.sin(angles))[:, None] + current_north[None, :]) * courant_scale / divisor, -courant_limit, courant_limit)
        pos_x = jnp.maximum(along_x, 0.0)
        neg_x = jnp.minimum(along_x, 0.0)
        pos_y = jnp.maximum(along_y, 0.0)
        neg_y = jnp.minimum(along_y, 0.0)
        for repeat in range(SUB):
            padded = jnp.pad(values, ((0, 0), (HALO, HALO)))
            west_value = padded[:, global_index[0]]
            east_value = padded[:, global_index[1]]
            south_value = padded[:, global_index[2]]
            north_value = padded[:, global_index[3]]
            updated = values - pos_x * (values - west_value) - neg_x * (east_value - values) - pos_y * (values - south_value) - neg_y * (north_value - values)
            values = jnp.where(repeat < counts[:, None], updated, values)
        return values

    def propagate(spectra):
        shaped = spectra.reshape(NF, ND, PTS)
        moved = lax.map(per_frequency, (shaped, wave_speed, substeps.reshape(NF, ND)))
        return moved.reshape(NF * ND, PTS)

    def source_term(spectra):
        spectra_grid = spectra.reshape(NF, ND, PTS)
        rounded = spectra_grid.astype(jnp.bfloat16)

        def accumulate(total, index):
            matrix = blocks[index].astype(jnp.float32)
            first_freq = quad_index[0, index]
            second_freq = quad_index[1, index]
            third_freq = quad_index[2, index]
            target = quad_index[3, index]
            left_term = jnp.dot(matrix, rounded[first_freq].astype(jnp.float32), precision=lax.Precision.HIGHEST)
            right_term = jnp.dot(matrix.T, rounded[second_freq].astype(jnp.float32), precision=lax.Precision.HIGHEST)
            product = (left_term * right_term * spectra_grid[third_freq]).astype(jnp.bfloat16)
            part_term = jnp.dot(matrix, product.astype(jnp.float32), precision=lax.Precision.HIGHEST)
            return total.at[target].add(strength[index] * part_term), None

        total, unused = lax.scan(accumulate, jnp.zeros((NF, ND, PTS), jnp.float32), jnp.arange(NBLK, dtype=jnp.int32))
        return (spectra_grid + source_step * total).reshape(NF * ND, PTS)

    spectra = spectrum
    for repeat in range(STEPS):
        spectra = source_term(propagate(spectra))
    return spectra
```

```python
import functools
import math

import jax
import jax.numpy as jnp
from jax import lax
from jax.experimental import pallas as pl
from jax.experimental.pallas import tpu as pltpu
from jax.sharding import PartitionSpec as P

NF = 36
ND = 64
SUB = 4
HALO = 128
DEEP = SUB * HALO
LANES = 128
TILES = DEEP // LANES

courant_scale = 0.4
courant_limit = 0.45
source_step = 0.1

VMEM = pl.BlockSpec(memory_space=pltpu.VMEM)
SMEM = pl.BlockSpec(memory_space=pltpu.SMEM)
PARAMS = pltpu.CompilerParams(vmem_limit_bytes=56 << 20)


def split(values):
    high = values.astype(jnp.bfloat16)
    return high, (values - high.astype(jnp.float32)).astype(jnp.bfloat16)


def lane_tile(t, width=1):
    return pl.ds(pl.multiple_of(t * LANES, LANES), width * LANES)


def propagate_kernel(turn, left, own, right, table, rows, *refs):
    outs, (field, parts, courant, pick) = refs[:TILES], refs[TILES:]
    count = own.shape[0]
    total = 3 * TILES
    position = lax.broadcasted_iota(jnp.int32, (2 * LANES, LANES), 0).astype(jnp.float32)

    def build(t, carry):
        cols = lane_tile(t)
        for side in range(2):
            for d in range(2):
                chosen = position == table[2 * d + side : 2 * d + side + 1, cols]
                pick[t, side, :, d * LANES : (d + 1) * LANES] = jnp.where(chosen, 1.0, 0.0).astype(jnp.bfloat16)
        return carry

    lax.fori_loop(1, total - 1, build, 0)
    for j, ref in enumerate((left, own, right)):
        cols = slice(j * DEEP, (j + 1) * DEEP)
        values = ref[...]
        field[:, cols] = values
        parts[0, :count, cols], parts[0, count:, cols] = split(values)
    east, north, inverse, substeps = (jnp.broadcast_to(rows[:, c : c + 1], (count, LANES)) for c in range(4))

    def courants(t, carry):
        cols = lane_tile(t)
        limit = table[6:7, cols]
        courant[t, 0] = jnp.clip(east + inverse * table[4:5, cols], -limit, limit)
        courant[t, 1] = jnp.clip(north + inverse * table[5:6, cols], -limit, limit)
        return carry

    lax.fori_loop(1, total - 1, courants, 0)
    for s in range(SUB):
        source, target = s % 2, 1 - s % 2

        def sweep(t, carry):
            behind = jnp.dot(parts[source, :, lane_tile(t - 1, 2)], pick[t, 0], preferred_element_type=jnp.float32)
            ahead = jnp.dot(parts[source, :, lane_tile(t, 2)], pick[t, 1], preferred_element_type=jnp.float32)
            behind = behind[:count] + behind[count:]
            ahead = ahead[:count] + ahead[count:]
            cols = lane_tile(t)
            values = field[:, cols]
            updated = values
            for d in range(2):
                speed = courant[t, d]
                half = slice(d * LANES, (d + 1) * LANES)
                upwind = jnp.where(speed > 0, behind[:, half], ahead[:, half])
                updated = updated - jnp.abs(speed) * (values - upwind)
            if s:
                updated = jnp.where(substeps > s, updated, values)
            field[:, cols] = updated
            if s < SUB - 1:
                parts[target, :count, cols], parts[target, count:, cols] = split(updated)
            return carry

        lax.fori_loop(s + 1, total - 1 - s, sweep, 0)
    for m, out in enumerate(outs):
        tile = lax.rem(turn[0] + m, TILES)
        out[...] = field[:, lane_tile(tile + TILES)]


def propagate(turn, left, own, right, table, rows):
    count = own.shape[0]
    return pl.pallas_call(
        propagate_kernel,
        out_shape=[jax.ShapeDtypeStruct((count, LANES), jnp.float32)] * TILES,
        in_specs=[SMEM] + [VMEM] * 5,
        out_specs=[VMEM] * TILES,
        scratch_shapes=[
            pltpu.VMEM((count, 3 * DEEP), jnp.float32),
            pltpu.VMEM((2, 2 * count, 3 * DEEP), jnp.bfloat16),
            pltpu.VMEM((3 * TILES, 2, count, LANES), jnp.float32),
            pltpu.VMEM((3 * TILES, 2, 2 * LANES, 2 * LANES), jnp.bfloat16),
        ],
        compiler_params=PARAMS,
        name="propagate",
    )(turn, left, own, right, table, rows)


def source_kernel(starts, step, arrived, quad, strength, turn, blocks, turned, *refs):
    ins, outs, (field, rounded, total) = refs[:arrived], refs[arrived:-3], refs[-3:]
    peers = len(outs)
    row_count = field.shape[0] // peers
    for m, group in enumerate(starts):
        base = lax.rem(turn[0] + peers - m, peers) * row_count
        for offset, ref in zip(group, ins[m * len(group) : (m + 1) * len(group)]):
            rows = pl.ds(pl.multiple_of(base + offset, 16), ref.shape[0])
            values = ref[...]
            field[rows, :] = values
            total[rows, :] = values
            rounded[rows, :] = values.astype(jnp.bfloat16)

    def rows_of(f):
        return pl.ds(pl.multiple_of(f * ND, ND), ND)

    def some(g, carry):
        products = []
        for k in range(step):
            j = g * step + k
            left = jnp.dot(blocks[j], rounded[rows_of(quad[0, j]), :], preferred_element_type=jnp.float32)
            right = jnp.dot(turned[j], rounded[rows_of(quad[1, j]), :], preferred_element_type=jnp.float32)
            products.append((left * right * field[rows_of(quad[2, j]), :]).astype(jnp.bfloat16))
        for k in range(step):
            j = g * step + k
            part = jnp.dot(blocks[j], products[k], preferred_element_type=jnp.float32)
            rows = rows_of(quad[3, j])
            total[rows, :] += (source_step * strength[j]) * part
        return carry

    lax.fori_loop(0, blocks.shape[0] // step, some, 0)
    for m, out in enumerate(outs):
        base = lax.rem(turn[0] + m, peers) * row_count
        out[...] = total[pl.ds(pl.multiple_of(base, 8), row_count), :]


def source_term(turn, pieces, starts, quad_index, strength, blocks, turned, peers):
    columns = pieces[0].shape[1]
    row_count = NF * ND // peers
    step = math.gcd(blocks.shape[0], 8)
    return pl.pallas_call(
        functools.partial(source_kernel, starts, step, len(pieces)),
        out_shape=[jax.ShapeDtypeStruct((row_count, columns), jnp.float32)] * peers,
        in_specs=[SMEM] * 3 + [VMEM] * (2 + len(pieces)),
        out_specs=[VMEM] * peers,
        scratch_shapes=[
            pltpu.VMEM((NF * ND, columns), jnp.float32),
            pltpu.VMEM((NF * ND, columns), jnp.bfloat16),
            pltpu.VMEM((NF * ND, columns), jnp.float32),
        ],
        compiler_params=PARAMS,
        name="source",
    )(quad_index, strength, turn, blocks, turned, *pieces)


def gather_kernel(turn, *refs):
    ins, out = refs[:-1], refs[-1]
    peers = len(ins)
    for m, ref in enumerate(ins):
        tile = lax.rem(turn[0] + peers - m, peers)
        out[:, lane_tile(tile)] = ref[...]


def gather_columns(turn, pieces):
    rows, columns = pieces[0].shape
    return pl.pallas_call(
        gather_kernel,
        out_shape=jax.ShapeDtypeStruct((rows, columns * len(pieces)), jnp.float32),
        in_specs=[SMEM] + [VMEM] * len(pieces),
        out_specs=VMEM,
        compiler_params=PARAMS,
        name="columns",
    )(turn, *pieces)


def from_sides(cells, width):
    count = lax.axis_size("space")
    head, tail = cells[:, :width], cells[:, cells.shape[1] - width :]
    before = lax.ppermute(tail, "space", [(i, i + 1) for i in range(count - 1)])
    after = lax.ppermute(head, "space", [(i + 1, i) for i in range(count - 1)])
    return before, after


def point_table(neighbours, current_east, current_north):
    columns = neighbours.shape[1]
    tile = jnp.arange(columns, dtype=jnp.int32) // LANES * LANES
    west, east, south, north = neighbours
    return jnp.stack(
        [
            (west - tile).astype(jnp.float32),
            (east - tile - LANES).astype(jnp.float32),
            (south - tile).astype(jnp.float32),
            (north - tile - LANES).astype(jnp.float32),
            current_east,
            current_north,
            jnp.full((columns,), courant_limit, jnp.float32),
            jnp.zeros((columns,), jnp.float32),
        ]
    )


def row_table(first_comp, row_count, substeps, wave_speed):
    angles = (jnp.arange(ND, dtype=jnp.float32) + 0.5) * (2.0 * math.pi / ND)
    inverse = courant_scale / substeps.astype(jnp.float32)
    speed = wave_speed[:, None]
    along = [(speed * turn(angles)[None, :]).reshape(NF * ND) * inverse for turn in (jnp.cos, jnp.sin)]
    table = jnp.stack(along + [inverse, substeps.astype(jnp.float32)], axis=1)
    return lax.dynamic_slice_in_dim(table, first_comp, row_count)


def cuts_of(row_count):
    if row_count % 192:
        return [(0, row_count)]
    first = 192
    return [(0, first), (first, row_count)] if row_count > first else [(0, row_count)]


def shards(
    spectrum,
    wave_speed,
    current_east,
    current_north,
    substeps,
    neighbours,
    blocks,
    quad_index,
    strength,
):
    peers = lax.axis_size("comp")
    row_count, columns = spectrum.shape
    own_index = lax.axis_index("comp").astype(jnp.int32)
    turn = own_index.reshape(1)
    table = point_table(neighbours, current_east, current_north)
    table = jnp.concatenate([from_sides(table, DEEP)[0], table, from_sides(table, DEEP)[1]], axis=1)
    rows = row_table(own_index * row_count, row_count, substeps, wave_speed)
    turned = blocks.swapaxes(1, 2)
    if columns == DEEP and peers == TILES:
        cuts = cuts_of(row_count)
        sent = [[] for _ in range(peers)]
        for low, high in cuts:
            chunk = spectrum[low:high]
            before, after = from_sides(chunk, DEEP)
            moved = propagate(turn, before, chunk, after, table, rows[low:high])
            for m in range(peers):
                piece = moved[m]
                if m:
                    piece = lax.ppermute(piece, "comp", [(i, (i + m) % peers) for i in range(peers)])
                sent[m].append(piece)
        pieces = [piece for group in sent for piece in group]
        starts = [[low for low, high in cuts]] * peers
        results = source_term(turn, pieces, starts, quad_index, strength, blocks, turned, peers)
        back = [
            lax.ppermute(piece, "comp", [(i, (i + m) % peers) for i in range(peers)]) if m else piece
            for m, piece in enumerate(results)
        ]
        return gather_columns(turn, back)
    still = jnp.zeros((1,), jnp.int32)
    extra = -row_count % 16
    chunk = jnp.pad(spectrum, ((0, extra), (0, 0)))
    rows = jnp.pad(rows, ((0, extra), (0, 0)))
    before, after = from_sides(chunk, DEEP)
    wide = jnp.concatenate([before, chunk, after], axis=1)
    tiles = []
    for first in range(0, columns, DEEP):
        near = [wide[:, first + j * DEEP : first + (j + 1) * DEEP] for j in range(3)]
        tiles += propagate(still, *near, table[:, first : first + 3 * DEEP], rows)
    grid = jnp.concatenate(tiles, axis=1)[:row_count].reshape(row_count, peers, columns // peers).swapaxes(0, 1)
    arrived = lax.all_to_all(grid, "comp", 0, 0, tiled=True)
    arrived = arrived.reshape(NF * ND, columns // peers)
    (results,) = source_term(still, [arrived], [[0]], quad_index, strength, blocks, turned, 1)
    results = results.reshape(peers, row_count, columns // peers)
    back = lax.all_to_all(results, "comp", 0, 0, tiled=True)
    return back.swapaxes(0, 1).reshape(row_count, columns)


def solution(mesh):
    in_specs = (
        P("comp", ("grp", "space")),
        P(),
        P(("grp", "space")),
        P(("grp", "space")),
        P(),
        P(None, ("grp", "space")),
        P(),
        P(),
        P(),
    )
    out_specs = P("comp", ("grp", "space"))
    return jax.shard_map(shards, mesh=mesh, in_specs=in_specs, out_specs=out_specs, check_vma=False)
```

```python
import functools
import math

import jax
import jax.numpy as jnp
from jax import lax
from jax.experimental import pallas as pl
from jax.experimental.pallas import tpu as pltpu
from jax.sharding import PartitionSpec as P

NF = 36
ND = 64
SUB = 4
HALO = 128
DEEP = SUB * HALO
LANES = 128
TILES = DEEP // LANES

courant_scale = 0.4
courant_limit = 0.45
source_step = 0.1

VMEM = pl.BlockSpec(memory_space=pltpu.VMEM)
SMEM = pl.BlockSpec(memory_space=pltpu.SMEM)
ANY = pl.BlockSpec(memory_space=pl.ANY)
PARAMS = pltpu.CompilerParams(vmem_limit_bytes=56 << 20)


def split(values):
    high = values.astype(jnp.bfloat16)
    return high, (values - high.astype(jnp.float32)).astype(jnp.bfloat16)


def lane_tile(t, width=1):
    if isinstance(t, int):
        return slice(t * LANES, (t + width) * LANES)
    return pl.ds(pl.multiple_of(t * LANES, LANES), width * LANES)


def copy_all(pairs, flags):
    copies = [pltpu.make_async_copy(source, target, flags.at[i]) for i, (source, target) in enumerate(pairs)]
    for copy in copies:
        copy.start()
    return copies


def propagate_kernel(first, low, turn, rows, *refs):
    tables, sides, outs = refs[:3], refs[3:6], refs[6 : 6 + TILES]
    table, field, parts_a, parts_b, along_x, along_y, behind_pick, ahead_pick, flags = refs[6 + TILES :]
    parts = (parts_a, parts_b)
    count = field.shape[0]
    total = 3 * TILES
    pairs = [(ref.at[0:8, :], table.at[:, j * DEEP : (j + 1) * DEEP]) for j, ref in enumerate(tables)]
    pairs += [(ref.at[first : first + count, :], field.at[:, j * DEEP : (j + 1) * DEEP]) for j, ref in enumerate(sides)]
    copies = copy_all(pairs, flags)
    columns = jnp.transpose(rows[...])[low : low + count]
    east, north, inverse, substeps = (jnp.broadcast_to(columns[:, c : c + 1], (count, LANES)) for c in range(4))
    position = lax.broadcasted_iota(jnp.int32, (2 * LANES, LANES), 0).astype(jnp.float32)
    for copy in copies:
        copy.wait()
    parts_a[:count], parts_a[count:] = split(field[...])
    for s in range(SUB):
        source, target = parts[s % 2], parts[1 - s % 2]
        for t in range(s + 1, total - 1 - s):
            cols = lane_tile(t)
            if s == 0:
                for pick, side in ((behind_pick, 0), (ahead_pick, 1)):
                    for d in range(2):
                        chosen = position == table[2 * d + side : 2 * d + side + 1, cols]
                        pick[t, :, lane_tile(d)] = jnp.where(chosen, 1.0, 0.0).astype(jnp.bfloat16)
                limit = table[6:7, cols]
                along_x[t] = jnp.clip(east + inverse * table[4:5, cols], -limit, limit)
                along_y[t] = jnp.clip(north + inverse * table[5:6, cols], -limit, limit)
            behind = jnp.dot(source[:, lane_tile(t - 1, 2)], behind_pick[t], preferred_element_type=jnp.float32)
            ahead = jnp.dot(source[:, lane_tile(t, 2)], ahead_pick[t], preferred_element_type=jnp.float32)
            behind = behind[:count] + behind[count:]
            ahead = ahead[:count] + ahead[count:]
            values = field[:, cols]
            updated = values
            for d, along in enumerate((along_x, along_y)):
                speed = along[t]
                upwind = jnp.where(speed > 0, behind[:, lane_tile(d)], ahead[:, lane_tile(d)])
                updated = updated - jnp.abs(speed) * (values - upwind)
            if s:
                updated = jnp.where(substeps > s, updated, values)
            field[:, cols] = updated
            if s < SUB - 1:
                target[:count, cols], target[count:, cols] = split(updated)
    pairs = [
        (field.at[:, lane_tile(lax.rem(turn[0] + m, TILES) + TILES)], out) for m, out in enumerate(outs)
    ]
    for copy in copy_all(pairs, flags):
        copy.wait()


def propagate(turn, rows, tables, sides, first, low, count):
    total = 3 * TILES
    return pl.pallas_call(
        functools.partial(propagate_kernel, first, low),
        out_shape=[jax.ShapeDtypeStruct((count, LANES), jnp.float32)] * TILES,
        in_specs=[SMEM, VMEM] + [ANY] * 6,
        out_specs=[ANY] * TILES,
        scratch_shapes=[
            pltpu.VMEM((8, 3 * DEEP), jnp.float32),
            pltpu.VMEM((count, 3 * DEEP), jnp.float32),
            pltpu.VMEM((2 * count, 3 * DEEP), jnp.bfloat16),
            pltpu.VMEM((2 * count, 3 * DEEP), jnp.bfloat16),
            pltpu.VMEM((total, count, LANES), jnp.float32),
            pltpu.VMEM((total, count, LANES), jnp.float32),
            pltpu.VMEM((total, 2 * LANES, 2 * LANES), jnp.bfloat16),
            pltpu.VMEM((total, 2 * LANES, 2 * LANES), jnp.bfloat16),
            pltpu.SemaphoreType.DMA((6,)),
        ],
        compiler_params=PARAMS,
        name="propagate",
    )(turn, rows, *tables, *sides)


def source_kernel(starts, step, arrived, quad, strength, turn, blocks, turned, *refs):
    ins, outs, (field, rounded, total, flags) = refs[:arrived], refs[arrived:-4], refs[-4:]
    peers = len(outs)
    row_count = field.shape[0] // peers
    pairs = []
    for m, group in enumerate(starts):
        base = lax.rem(turn[0] + peers - m, peers) * row_count
        for offset, ref in zip(group, ins[m * len(group) : (m + 1) * len(group)]):
            pairs.append((ref, field.at[pl.ds(pl.multiple_of(base + offset, 8), ref.shape[0]), :]))
    for copy in copy_all(pairs, flags):
        copy.wait()
    values = field[...]
    total[...] = values
    rounded[...] = values.astype(jnp.bfloat16)

    def rows_of(f):
        return pl.ds(pl.multiple_of(f * ND, ND), ND)

    def some(g, carry):
        products = []
        for k in range(step):
            j = g * step + k
            left = jnp.dot(blocks[j], rounded[rows_of(quad[0, j]), :], preferred_element_type=jnp.float32)
            right = jnp.dot(turned[j], rounded[rows_of(quad[1, j]), :], preferred_element_type=jnp.float32)
            products.append((left * right * field[rows_of(quad[2, j]), :]).astype(jnp.bfloat16))
        for k in range(step):
            j = g * step + k
            part = jnp.dot(blocks[j], products[k], preferred_element_type=jnp.float32)
            rows = rows_of(quad[3, j])
            total[rows, :] += (source_step * strength[j]) * part
        return carry

    lax.fori_loop(0, blocks.shape[0] // step, some, 0)
    pairs = []
    for m, out in enumerate(outs):
        base = lax.rem(turn[0] + m, peers) * row_count
        pairs.append((total.at[pl.ds(pl.multiple_of(base, 8), row_count), :], out))
    for copy in copy_all(pairs, flags):
        copy.wait()


def source_term(turn, pieces, starts, quad_index, strength, blocks, turned, peers):
    columns = pieces[0].shape[1]
    row_count = NF * ND // peers
    step = math.gcd(blocks.shape[0], 8)
    return pl.pallas_call(
        functools.partial(source_kernel, starts, step, len(pieces)),
        out_shape=[jax.ShapeDtypeStruct((row_count, columns), jnp.float32)] * peers,
        in_specs=[SMEM] * 3 + [VMEM] * 2 + [ANY] * len(pieces),
        out_specs=[ANY] * peers,
        scratch_shapes=[
            pltpu.VMEM((NF * ND, columns), jnp.float32),
            pltpu.VMEM((NF * ND, columns), jnp.bfloat16),
            pltpu.VMEM((NF * ND, columns), jnp.float32),
            pltpu.SemaphoreType.DMA((max(len(pieces), peers),)),
        ],
        compiler_params=PARAMS,
        name="source",
    )(quad_index, strength, turn, blocks, turned, *pieces)


def gather_kernel(turn, *refs):
    ins, out, flags = refs[:-2], refs[-2], refs[-1]
    peers = len(ins)
    pairs = [(ref, out.at[:, lane_tile(lax.rem(turn[0] + peers - m, peers))]) for m, ref in enumerate(ins)]
    for copy in copy_all(pairs, flags):
        copy.wait()


def gather_columns(turn, pieces):
    rows, columns = pieces[0].shape
    return pl.pallas_call(
        gather_kernel,
        out_shape=jax.ShapeDtypeStruct((rows, columns * len(pieces)), jnp.float32),
        in_specs=[SMEM] + [ANY] * len(pieces),
        out_specs=ANY,
        scratch_shapes=[pltpu.SemaphoreType.DMA((len(pieces),))],
        compiler_params=PARAMS,
        name="columns",
    )(turn, *pieces)


def from_sides(cells, width):
    count = lax.axis_size("space")
    head, tail = cells[:, :width], cells[:, cells.shape[1] - width :]
    before = lax.ppermute(tail, "space", [(i, i + 1) for i in range(count - 1)])
    after = lax.ppermute(head, "space", [(i + 1, i) for i in range(count - 1)])
    return before, after


def point_table(neighbours, current_east, current_north):
    columns = neighbours.shape[1]
    tile = jnp.arange(columns, dtype=jnp.int32) // LANES * LANES
    west, east, south, north = neighbours
    return jnp.stack(
        [
            (west - tile).astype(jnp.float32),
            (east - tile - LANES).astype(jnp.float32),
            (south - tile).astype(jnp.float32),
            (north - tile - LANES).astype(jnp.float32),
            current_east,
            current_north,
            jnp.full((columns,), courant_limit, jnp.float32),
            jnp.zeros((columns,), jnp.float32),
        ]
    )


def row_table(first_comp, row_count, substeps, wave_speed):
    angles = (jnp.arange(ND, dtype=jnp.float32) + 0.5) * (2.0 * math.pi / ND)
    inverse = courant_scale / substeps.astype(jnp.float32)
    speed = wave_speed[:, None]
    along = [(speed * wave(angles)[None, :]).reshape(NF * ND) * inverse for wave in (jnp.cos, jnp.sin)]
    table = jnp.stack(along + [inverse, substeps.astype(jnp.float32)])
    own = lax.dynamic_slice_in_dim(table, first_comp, row_count, axis=1)
    return jnp.pad(own, ((0, 4), (0, -row_count % LANES)))


def cuts_of(row_count):
    middle = row_count // 2 // 16 * 16
    return [(0, middle), (middle, row_count)]


def shards(
    spectrum,
    wave_speed,
    current_east,
    current_north,
    substeps,
    neighbours,
    blocks,
    quad_index,
    strength,
):
    peers = lax.axis_size("comp")
    row_count, columns = spectrum.shape
    own_index = lax.axis_index("comp").astype(jnp.int32)
    turn = own_index.reshape(1)
    table = point_table(neighbours, current_east, current_north)
    rows = row_table(own_index * row_count, row_count, substeps, wave_speed)
    turned = blocks.swapaxes(1, 2)
    if columns == DEEP and peers == TILES and row_count % 16 == 0:
        cuts = cuts_of(row_count)
        sent = [[] for _ in range(peers)]
        tables, moved = None, None
        for low, high in cuts:
            chunk = spectrum[low:high]
            if tables is None:
                chunk = jnp.concatenate([table, chunk])
            else:
                chunk, *tables = lax.optimization_barrier((chunk, *tables))
            before, after = from_sides(chunk, DEEP)
            sides = (before, chunk, after)
            first = 0 if tables else 8
            tables = tables or sides
            moved = propagate(turn, rows, tables, sides, first, low, high - low)
            if sent[1]:
                arrived = [group[-1] for group in sent[1:]]
                held = lax.optimization_barrier((*moved, *arrived))
                moved = held[:peers]
                for group, piece in zip(sent[1:], held[peers:]):
                    group[-1] = piece
            for m in range(peers):
                piece = moved[m]
                if m:
                    piece = lax.ppermute(piece, "comp", [(i, (i + m) % peers) for i in range(peers)])
                sent[m].append(piece)
        pieces = [piece for group in sent for piece in group]
        starts = [[low for low, high in cuts]] * peers
        results = source_term(turn, pieces, starts, quad_index, strength, blocks, turned, peers)
        back = [
            lax.ppermute(piece, "comp", [(i, (i + m) % peers) for i in range(peers)]) if m else piece
            for m, piece in enumerate(results)
        ]
        return gather_columns(turn, back)
    still = jnp.zeros((1,), jnp.int32)
    extra = -row_count % 16
    chunk = jnp.pad(spectrum, ((0, extra), (0, 0)))
    before, after = from_sides(chunk, DEEP)
    wide = jnp.concatenate([before, chunk, after], axis=1)
    before, after = from_sides(table, DEEP)
    table = jnp.concatenate([before, table, after], axis=1)
    tiles = []
    for start in range(0, columns, DEEP):
        sides = [wide[:, start + j * DEEP : start + (j + 1) * DEEP] for j in range(3)]
        tables = [table[:, start + j * DEEP : start + (j + 1) * DEEP] for j in range(3)]
        tiles += propagate(still, rows, tables, sides, 0, 0, row_count + extra)
    grid = jnp.concatenate(tiles, axis=1)[:row_count].reshape(row_count, peers, columns // peers).swapaxes(0, 1)
    arrived = lax.all_to_all(grid, "comp", 0, 0, tiled=True)
    arrived = arrived.reshape(NF * ND, columns // peers)
    (results,) = source_term(still, [arrived], [[0]], quad_index, strength, blocks, turned, 1)
    results = results.reshape(peers, row_count, columns // peers)
    back = lax.all_to_all(results, "comp", 0, 0, tiled=True)
    return back.swapaxes(0, 1).reshape(row_count, columns)


def solution(mesh):
    in_specs = (
        P("comp", ("grp", "space")),
        P(),
        P(("grp", "space")),
        P(("grp", "space")),
        P(),
        P(None, ("grp", "space")),
        P(),
        P(),
        P(),
    )
    out_specs = P("comp", ("grp", "space"))
    return jax.shard_map(shards, mesh=mesh, in_specs=in_specs, out_specs=out_specs, check_vma=False)
```

```python
import functools
import math

import jax
import jax.numpy as jnp
from jax import lax
from jax.experimental import pallas as pl
from jax.experimental.pallas import tpu as pltpu
from jax.sharding import PartitionSpec as P

NF = 36
ND = 64
SUB = 4
HALO = 128
DEEP = SUB * HALO
LANES = 128
TILES = DEEP // LANES

courant_scale = 0.4
courant_limit = 0.45
source_step = 0.1

VMEM = pl.BlockSpec(memory_space=pltpu.VMEM)
SMEM = pl.BlockSpec(memory_space=pltpu.SMEM)
PARAMS = pltpu.CompilerParams(vmem_limit_bytes=40 << 20)


def in_vmem(values):
    return pltpu.with_memory_space_constraint(values, pltpu.VMEM)


def split(values):
    high = values.astype(jnp.bfloat16)
    return high, (values - high.astype(jnp.float32)).astype(jnp.bfloat16)


def lane_tile(t, width=1):
    if isinstance(t, int):
        return slice(t * LANES, (t + width) * LANES)
    return pl.ds(pl.multiple_of(t * LANES, LANES), width * LANES)


def propagate_kernel(first, low, turn, odd, rows, *refs):
    tables, sides, outs = refs[:3], refs[3:6], refs[6 : 6 + TILES]
    field, parts_a, parts_b, along_x, along_y, behind_pick, ahead_pick = refs[6 + TILES :]
    parts = (parts_a, parts_b)
    count = field.shape[0]
    total = 3 * TILES
    turned = odd[0] == 1
    columns = jnp.transpose(rows[...])[low : low + count]
    east, north, inverse, substeps = (jnp.broadcast_to(columns[:, c : c + 1], (count, LANES)) for c in range(4))
    position = lax.broadcasted_iota(jnp.int32, (2 * LANES, LANES), 0).astype(jnp.float32)

    def region(group, taken, t):
        cols = lane_tile(t % TILES)
        near, own, far = (ref[taken, cols] for ref in group)
        if t < TILES:
            return jnp.where(turned, near, far)
        return own if t < 2 * TILES else jnp.where(turned, far, near)

    def prepare(t):
        values = region(sides, slice(first, first + count), t)
        field[:, lane_tile(t)] = values
        parts_a[:count, lane_tile(t)], parts_a[count:, lane_tile(t)] = split(values)
        if 0 < t < total - 1:
            table = region(tables, slice(0, 8), t)
            for pick, side in ((behind_pick, 0), (ahead_pick, 1)):
                for d in range(2):
                    chosen = position == table[2 * d + side : 2 * d + side + 1]
                    pick[t, :, lane_tile(d)] = jnp.where(chosen, 1.0, 0.0).astype(jnp.bfloat16)
            limit = table[6:7]
            along_x[t] = jnp.clip(east + inverse * table[4:5], -limit, limit)
            along_y[t] = jnp.clip(north + inverse * table[5:6], -limit, limit)

    prepare(0)
    prepare(1)
    for s in range(SUB):
        source, target = parts[s % 2], parts[1 - s % 2]
        for t in range(s + 1, total - 1 - s):
            cols = lane_tile(t)
            if s == 0:
                prepare(t + 1)
            behind = jnp.dot(source[:, lane_tile(t - 1, 2)], behind_pick[t], preferred_element_type=jnp.float32)
            ahead = jnp.dot(source[:, lane_tile(t, 2)], ahead_pick[t], preferred_element_type=jnp.float32)
            behind = behind[:count] + behind[count:]
            ahead = ahead[:count] + ahead[count:]
            values = field[:, cols]
            updated = values
            for d, along in enumerate((along_x, along_y)):
                speed = along[t]
                upwind = jnp.where(speed > 0, behind[:, lane_tile(d)], ahead[:, lane_tile(d)])
                updated = updated - jnp.abs(speed) * (values - upwind)
            if s:
                updated = jnp.where(substeps > s, updated, values)
            field[:, cols] = updated
            if s < SUB - 1:
                target[:count, cols], target[count:, cols] = split(updated)
    for m, out in enumerate(outs):
        out[...] = field[:, lane_tile(lax.rem(turn[0] + m, TILES) + TILES)]


def propagate(turn, odd, rows, tables, sides, first, low, count):
    total = 3 * TILES
    return pl.pallas_call(
        functools.partial(propagate_kernel, first, low),
        out_shape=[pltpu.VMEM((count, LANES), jnp.float32)] * TILES,
        in_specs=[SMEM] * 2 + [VMEM] * 7,
        out_specs=[VMEM] * TILES,
        scratch_shapes=[
            pltpu.VMEM((count, 3 * DEEP), jnp.float32),
            pltpu.VMEM((2 * count, 3 * DEEP), jnp.bfloat16),
            pltpu.VMEM((2 * count, 3 * DEEP), jnp.bfloat16),
            pltpu.VMEM((total, count, LANES), jnp.float32),
            pltpu.VMEM((total, count, LANES), jnp.float32),
            pltpu.VMEM((total, 2 * LANES, 2 * LANES), jnp.bfloat16),
            pltpu.VMEM((total, 2 * LANES, 2 * LANES), jnp.bfloat16),
        ],
        compiler_params=PARAMS,
        name="propagate",
    )(turn, odd, in_vmem(rows), *map(in_vmem, tables), *map(in_vmem, sides))


def source_kernel(starts, step, arrived, quad, strength, turn, blocks, turned, *refs):
    ins, outs, (field, rounded, total) = refs[:arrived], refs[arrived:-3], refs[-3:]
    peers = len(outs)
    row_count = field.shape[0] // peers
    for m, group in enumerate(starts):
        base = lax.rem(turn[0] + peers - m, peers) * row_count
        for offset, ref in zip(group, ins[m * len(group) : (m + 1) * len(group)]):
            rows = pl.ds(pl.multiple_of(base + offset, 16), ref.shape[0])
            values = ref[...]
            field[rows, :] = values
            total[rows, :] = values
            rounded[rows, :] = values.astype(jnp.bfloat16)

    def rows_of(f):
        return pl.ds(pl.multiple_of(f * ND, ND), ND)

    def some(g, carry):
        products = []
        for k in range(step):
            j = g * step + k
            left = jnp.dot(blocks[j], rounded[rows_of(quad[0, j]), :], preferred_element_type=jnp.float32)
            right = jnp.dot(turned[j], rounded[rows_of(quad[1, j]), :], preferred_element_type=jnp.float32)
            products.append((left * right * field[rows_of(quad[2, j]), :]).astype(jnp.bfloat16))
        for k in range(step):
            j = g * step + k
            part = jnp.dot(blocks[j], products[k], preferred_element_type=jnp.float32)
            rows = rows_of(quad[3, j])
            total[rows, :] += (source_step * strength[j]) * part
        return carry

    lax.fori_loop(0, blocks.shape[0] // step, some, 0)
    for m, out in enumerate(outs):
        base = lax.rem(turn[0] + m, peers) * row_count
        out[...] = total[pl.ds(pl.multiple_of(base, 8), row_count), :]


def source_term(turn, pieces, starts, quad_index, strength, blocks, turned, peers):
    columns = pieces[0].shape[1]
    row_count = NF * ND // peers
    step = math.gcd(blocks.shape[0], 16)
    return pl.pallas_call(
        functools.partial(source_kernel, starts, step, len(pieces)),
        out_shape=[pltpu.VMEM((row_count, columns), jnp.float32)] * peers,
        in_specs=[SMEM] * 3 + [VMEM] * (2 + len(pieces)),
        out_specs=[VMEM] * peers,
        scratch_shapes=[
            pltpu.VMEM((NF * ND, columns), jnp.float32),
            pltpu.VMEM((NF * ND, columns), jnp.bfloat16),
            pltpu.VMEM((NF * ND, columns), jnp.float32),
        ],
        compiler_params=PARAMS,
        name="source",
    )(quad_index, strength, turn, in_vmem(blocks), in_vmem(turned), *map(in_vmem, pieces))


def gather_kernel(turn, *refs):
    ins, out = refs[:-1], refs[-1]
    peers = len(ins)
    for m, ref in enumerate(ins):
        out[:, lane_tile(lax.rem(turn[0] + peers - m, peers))] = ref[...]


def gather_columns(turn, pieces):
    rows, columns = pieces[0].shape
    return pl.pallas_call(
        gather_kernel,
        out_shape=jax.ShapeDtypeStruct((rows, columns * len(pieces)), jnp.float32),
        in_specs=[SMEM] + [VMEM] * len(pieces),
        out_specs=VMEM,
        compiler_params=PARAMS,
        name="columns",
    )(turn, *map(in_vmem, pieces))


def from_sides(cells, width):
    count = lax.axis_size("space")
    head, tail = cells[:, :width], cells[:, cells.shape[1] - width :]
    before = lax.ppermute(tail, "space", [(i, i + 1) for i in range(count - 1)])
    after = lax.ppermute(head, "space", [(i + 1, i) for i in range(count - 1)])
    return before, after


def from_pairs(cells):
    count = lax.axis_size("space")
    pairs = [[], []]
    for i in range(count - 1):
        pairs[i % 2] += [(i, i + 1), (i + 1, i)]
    far = lax.ppermute(cells, "space", pairs[1])
    near = lax.ppermute(cells, "space", pairs[0])
    return near, cells, far


def point_table(neighbours, current_east, current_north):
    columns = neighbours.shape[1]
    tile = jnp.arange(columns, dtype=jnp.int32) // LANES * LANES
    west, east, south, north = neighbours
    return jnp.stack(
        [
            (west - tile).astype(jnp.float32),
            (east - tile - LANES).astype(jnp.float32),
            (south - tile).astype(jnp.float32),
            (north - tile - LANES).astype(jnp.float32),
            current_east,
            current_north,
            jnp.full((columns,), courant_limit, jnp.float32),
            jnp.zeros((columns,), jnp.float32),
        ]
    )


def row_table(first_comp, row_count, substeps, wave_speed):
    angles = (jnp.arange(ND, dtype=jnp.float32) + 0.5) * (2.0 * math.pi / ND)
    inverse = courant_scale / substeps.astype(jnp.float32)
    speed = wave_speed[:, None]
    along = [(speed * wave(angles)[None, :]).reshape(NF * ND) * inverse for wave in (jnp.cos, jnp.sin)]
    table = jnp.stack(along + [inverse, substeps.astype(jnp.float32)])
    own = lax.dynamic_slice_in_dim(table, first_comp, row_count, axis=1)
    return jnp.pad(own, ((0, 4), (0, -row_count % LANES)))


def cuts_of(row_count):
    middle = row_count // 2 // 16 * 16
    return [(0, middle), (middle, row_count)]


def shards(
    spectrum,
    wave_speed,
    current_east,
    current_north,
    substeps,
    neighbours,
    blocks,
    quad_index,
    strength,
):
    peers = lax.axis_size("comp")
    row_count, columns = spectrum.shape
    own_index = lax.axis_index("comp").astype(jnp.int32)
    turn = own_index.reshape(1)
    odd = lax.rem(lax.axis_index("space").astype(jnp.int32), 2).reshape(1)
    table = point_table(neighbours, current_east, current_north)
    rows = row_table(own_index * row_count, row_count, substeps, wave_speed)
    turned = blocks.swapaxes(1, 2)
    if columns == DEEP and peers == TILES and row_count % 16 == 0:
        cuts = cuts_of(row_count)
        sent = [[] for _ in range(peers)]
        tables, moved = None, None
        for low, high in cuts:
            chunk = spectrum[low:high]
            if tables is None:
                chunk = jnp.concatenate([table, chunk])
            else:
                chunk, *tables = lax.optimization_barrier((chunk, *tables))
            sides = from_pairs(chunk)
            first = 0 if tables else 8
            tables = tables or sides
            moved = propagate(turn, odd, rows, tables, sides, first, low, high - low)
            if sent[1]:
                arrived = [group[-1][:8] for group in sent[1:]]
                moved = lax.optimization_barrier((*moved, *arrived))[:peers]
            for m in range(peers):
                piece = moved[m]
                if m:
                    piece = lax.ppermute(piece, "comp", [(i, (i + m) % peers) for i in range(peers)])
                sent[m].append(piece)
        pieces = [piece for group in sent for piece in group]
        starts = [[low for low, high in cuts]] * peers
        results = source_term(turn, pieces, starts, quad_index, strength, blocks, turned, peers)
        back = [
            lax.ppermute(piece, "comp", [(i, (i + m) % peers) for i in range(peers)]) if m else piece
            for m, piece in enumerate(results)
        ]
        return gather_columns(turn, back)
    still = jnp.zeros((1,), jnp.int32)
    extra = -row_count % 16
    chunk = jnp.pad(spectrum, ((0, extra), (0, 0)))
    before, after = from_sides(chunk, DEEP)
    wide = jnp.concatenate([before, chunk, after], axis=1)
    before, after = from_sides(table, DEEP)
    table = jnp.concatenate([before, table, after], axis=1)
    tiles = []
    for start in range(0, columns, DEEP):
        sides = [wide[:, start + j * DEEP : start + (j + 1) * DEEP] for j in range(3)]
        tables = [table[:, start + j * DEEP : start + (j + 1) * DEEP] for j in range(3)]
        tiles += propagate(still, still + 1, rows, tables, sides, 0, 0, row_count + extra)
    grid = jnp.concatenate(tiles, axis=1)[:row_count].reshape(row_count, peers, columns // peers).swapaxes(0, 1)
    arrived = lax.all_to_all(grid, "comp", 0, 0, tiled=True)
    arrived = arrived.reshape(NF * ND, columns // peers)
    (results,) = source_term(still, [arrived], [[0]], quad_index, strength, blocks, turned, 1)
    results = results.reshape(peers, row_count, columns // peers)
    back = lax.all_to_all(results, "comp", 0, 0, tiled=True)
    return back.swapaxes(0, 1).reshape(row_count, columns)


def solution(mesh):
    in_specs = (
        P("comp", ("grp", "space")),
        P(),
        P(("grp", "space")),
        P(("grp", "space")),
        P(),
        P(None, ("grp", "space")),
        P(),
        P(),
        P(),
    )
    out_specs = P("comp", ("grp", "space"))
    return jax.shard_map(shards, mesh=mesh, in_specs=in_specs, out_specs=out_specs, check_vma=False)
```

```python
import functools
import math

import jax
import jax.numpy as jnp
from jax import lax
from jax.experimental import pallas as pl
from jax.experimental.pallas import tpu as pltpu
from jax.sharding import PartitionSpec as P

NF = 36
ND = 64
SUB = 4
HALO = 128
DEEP = SUB * HALO
LANES = 128
TILES = DEEP // LANES

courant_scale = 0.4
courant_limit = 0.45
source_step = 0.1

VMEM = pl.BlockSpec(memory_space=pltpu.VMEM)
SMEM = pl.BlockSpec(memory_space=pltpu.SMEM)
PARAMS = pltpu.CompilerParams(vmem_limit_bytes=40 << 20)


def in_vmem(values):
    return pltpu.with_memory_space_constraint(values, pltpu.VMEM)


def in_hbm(values):
    return pltpu.with_memory_space_constraint(values, pltpu.HBM)


def split(values):
    high = values.astype(jnp.bfloat16)
    return high, (values - high.astype(jnp.float32)).astype(jnp.bfloat16)


def lane_tile(t, width=1):
    if isinstance(t, int):
        return slice(t * LANES, (t + width) * LANES)
    return pl.ds(pl.multiple_of(t * LANES, LANES), width * LANES)


def propagate_kernel(first, low, turn, odd, rows, *refs):
    tables, sides, outs = refs[:3], refs[3:6], refs[6 : 6 + TILES]
    field, parts_a, parts_b, along_x, along_y, behind_pick, ahead_pick = refs[6 + TILES :]
    parts = (parts_a, parts_b)
    count = field.shape[0]
    total = 3 * TILES
    turned = odd[0] == 1
    columns = jnp.transpose(rows[...])[low : low + count]
    east, north, inverse, substeps = (jnp.broadcast_to(columns[:, c : c + 1], (count, LANES)) for c in range(4))
    position = lax.broadcasted_iota(jnp.int32, (2 * LANES, LANES), 0).astype(jnp.float32)

    def region(group, taken, t):
        cols = lane_tile(t % TILES)
        near, own, far = (ref[taken, cols] for ref in group)
        if t < TILES:
            return jnp.where(turned, near, far)
        return own if t < 2 * TILES else jnp.where(turned, far, near)

    def prepare(t):
        values = region(sides, slice(first, first + count), t)
        field[:, lane_tile(t)] = values
        parts_a[:count, lane_tile(t)], parts_a[count:, lane_tile(t)] = split(values)
        if 0 < t < total - 1:
            table = region(tables, slice(0, 8), t)
            for pick, side in ((behind_pick, 0), (ahead_pick, 1)):
                for d in range(2):
                    chosen = position == table[2 * d + side : 2 * d + side + 1]
                    pick[t, :, lane_tile(d)] = jnp.where(chosen, 1.0, 0.0).astype(jnp.bfloat16)
            limit = table[6:7]
            along_x[t] = jnp.clip(east + inverse * table[4:5], -limit, limit)
            along_y[t] = jnp.clip(north + inverse * table[5:6], -limit, limit)

    prepare(0)
    prepare(1)
    for s in range(SUB):
        source, target = parts[s % 2], parts[1 - s % 2]
        for t in range(s + 1, total - 1 - s):
            cols = lane_tile(t)
            if s == 0:
                prepare(t + 1)
            behind = jnp.dot(source[:, lane_tile(t - 1, 2)], behind_pick[t], preferred_element_type=jnp.float32)
            ahead = jnp.dot(source[:, lane_tile(t, 2)], ahead_pick[t], preferred_element_type=jnp.float32)
            behind = behind[:count] + behind[count:]
            ahead = ahead[:count] + ahead[count:]
            values = field[:, cols]
            updated = values
            for d, along in enumerate((along_x, along_y)):
                speed = along[t]
                upwind = jnp.where(speed > 0, behind[:, lane_tile(d)], ahead[:, lane_tile(d)])
                updated = updated - jnp.abs(speed) * (values - upwind)
            if s:
                updated = jnp.where(substeps > s, updated, values)
            field[:, cols] = updated
            if s < SUB - 1:
                target[:count, cols], target[count:, cols] = split(updated)
    for m, out in enumerate(outs):
        out[...] = field[:, lane_tile(lax.rem(turn[0] + m, TILES) + TILES)]


def propagate(turn, odd, rows, tables, sides, first, low, count):
    total = 3 * TILES
    return pl.pallas_call(
        functools.partial(propagate_kernel, first, low),
        out_shape=[jax.ShapeDtypeStruct((count, LANES), jnp.float32)] + [pltpu.VMEM((count, LANES), jnp.float32)] * (TILES - 1),
        in_specs=[SMEM] * 2 + [VMEM] * 7,
        out_specs=[VMEM] * TILES,
        scratch_shapes=[
            pltpu.VMEM((count, 3 * DEEP), jnp.float32),
            pltpu.VMEM((2 * count, 3 * DEEP), jnp.bfloat16),
            pltpu.VMEM((2 * count, 3 * DEEP), jnp.bfloat16),
            pltpu.VMEM((total, count, LANES), jnp.float32),
            pltpu.VMEM((total, count, LANES), jnp.float32),
            pltpu.VMEM((total, 2 * LANES, 2 * LANES), jnp.bfloat16),
            pltpu.VMEM((total, 2 * LANES, 2 * LANES), jnp.bfloat16),
        ],
        compiler_params=PARAMS,
        name="propagate",
    )(turn, odd, in_vmem(rows), *map(in_vmem, tables), *map(in_vmem, sides))


def source_kernel(starts, step, arrived, quad, strength, turn, blocks, turned, *refs):
    ins, outs, (field, rounded, total) = refs[:arrived], refs[arrived:-3], refs[-3:]
    peers = len(outs)
    row_count = field.shape[0] // peers
    for m, group in enumerate(starts):
        base = lax.rem(turn[0] + peers - m, peers) * row_count
        for offset, ref in zip(group, ins[m * len(group) : (m + 1) * len(group)]):
            rows = pl.ds(pl.multiple_of(base + offset, 16), ref.shape[0])
            values = ref[...]
            field[rows, :] = values
            total[rows, :] = values
            rounded[rows, :] = values.astype(jnp.bfloat16)

    def rows_of(f):
        return pl.ds(pl.multiple_of(f * ND, ND), ND)

    def some(g, carry):
        products = []
        for k in range(step):
            j = g * step + k
            left = jnp.dot(blocks[j], rounded[rows_of(quad[0, j]), :], preferred_element_type=jnp.float32)
            right = jnp.dot(turned[j], rounded[rows_of(quad[1, j]), :], preferred_element_type=jnp.float32)
            products.append((left * right * field[rows_of(quad[2, j]), :]).astype(jnp.bfloat16))
        for k in range(step):
            j = g * step + k
            part = jnp.dot(blocks[j], products[k], preferred_element_type=jnp.float32)
            rows = rows_of(quad[3, j])
            total[rows, :] += (source_step * strength[j]) * part
        return carry

    lax.fori_loop(0, blocks.shape[0] // step, some, 0)
    for m, out in enumerate(outs):
        base = lax.rem(turn[0] + m, peers) * row_count
        out[...] = total[pl.ds(pl.multiple_of(base, 8), row_count), :]


def source_term(turn, pieces, starts, quad_index, strength, blocks, turned, peers):
    columns = pieces[0].shape[1]
    row_count = NF * ND // peers
    step = math.gcd(blocks.shape[0], 16)
    return pl.pallas_call(
        functools.partial(source_kernel, starts, step, len(pieces)),
        out_shape=[pltpu.VMEM((row_count, columns), jnp.float32)] * peers,
        in_specs=[SMEM] * 3 + [VMEM] * (2 + len(pieces)),
        out_specs=[VMEM] * peers,
        scratch_shapes=[
            pltpu.VMEM((NF * ND, columns), jnp.float32),
            pltpu.VMEM((NF * ND, columns), jnp.bfloat16),
            pltpu.VMEM((NF * ND, columns), jnp.float32),
        ],
        compiler_params=PARAMS,
        name="source",
    )(quad_index, strength, turn, in_vmem(blocks), in_vmem(turned), *map(in_vmem, pieces))


def gather_kernel(turn, *refs):
    ins, out = refs[:-1], refs[-1]
    peers = len(ins)
    for m, ref in enumerate(ins):
        out[:, lane_tile(lax.rem(turn[0] + peers - m, peers))] = ref[...]


def gather_columns(turn, pieces):
    rows, columns = pieces[0].shape
    return pl.pallas_call(
        gather_kernel,
        out_shape=jax.ShapeDtypeStruct((rows, columns * len(pieces)), jnp.float32),
        in_specs=[SMEM] + [VMEM] * len(pieces),
        out_specs=VMEM,
        compiler_params=PARAMS,
        name="columns",
    )(turn, *map(in_vmem, pieces))


def from_sides(cells, width):
    count = lax.axis_size("space")
    head, tail = cells[:, :width], cells[:, cells.shape[1] - width :]
    before = lax.ppermute(tail, "space", [(i, i + 1) for i in range(count - 1)])
    after = lax.ppermute(head, "space", [(i + 1, i) for i in range(count - 1)])
    return before, after


def from_pairs(cells):
    count = lax.axis_size("space")
    pairs = [[], []]
    for i in range(count - 1):
        pairs[i % 2] += [(i, i + 1), (i + 1, i)]
    far = lax.ppermute(cells, "space", pairs[1])
    near = lax.ppermute(cells, "space", pairs[0])
    return near, cells, far


def point_table(neighbours, current_east, current_north):
    columns = neighbours.shape[1]
    tile = jnp.arange(columns, dtype=jnp.int32) // LANES * LANES
    west, east, south, north = neighbours
    return jnp.stack(
        [
            (west - tile).astype(jnp.float32),
            (east - tile - LANES).astype(jnp.float32),
            (south - tile).astype(jnp.float32),
            (north - tile - LANES).astype(jnp.float32),
            current_east,
            current_north,
            jnp.full((columns,), courant_limit, jnp.float32),
            jnp.zeros((columns,), jnp.float32),
        ]
    )


def pack_kernel(neighbours, east, north, cells, out):
    columns = out.shape[1]
    tile = lax.broadcasted_iota(jnp.int32, (4, columns), 1) // LANES * LANES
    ahead = lax.broadcasted_iota(jnp.int32, (4, columns), 0) % 2 * LANES
    out[0:4] = (neighbours[...] - tile - ahead).astype(jnp.float32)
    out[4:5] = east[...].reshape(1, columns)
    out[5:6] = north[...].reshape(1, columns)
    out[6:8] = jnp.full((2, columns), courant_limit, jnp.float32)
    out[8:] = cells[...]


def pack(neighbours, east, north, spectrum, count):
    columns = spectrum.shape[1]
    return pl.pallas_call(
        pack_kernel,
        grid=(1,),
        out_shape=pltpu.VMEM((8 + count, columns), jnp.float32),
        in_specs=[
            pl.BlockSpec((4, columns), lambda i: (0, 0)),
            pl.BlockSpec((1, columns), lambda i: (0, 0)),
            pl.BlockSpec((1, columns), lambda i: (0, 0)),
            pl.BlockSpec((count, columns), lambda i: (0, 0)),
        ],
        out_specs=pl.BlockSpec((8 + count, columns), lambda i: (0, 0)),
        compiler_params=PARAMS,
        name="pack",
    )(*map(in_hbm, (neighbours, east[None], north[None], spectrum)))


def row_table(first_comp, row_count, substeps, wave_speed):
    angles = (jnp.arange(ND, dtype=jnp.float32) + 0.5) * (2.0 * math.pi / ND)
    inverse = courant_scale / substeps.astype(jnp.float32)
    speed = wave_speed[:, None]
    along = [(speed * wave(angles)[None, :]).reshape(NF * ND) * inverse for wave in (jnp.cos, jnp.sin)]
    table = jnp.stack(along + [inverse, substeps.astype(jnp.float32)])
    own = lax.dynamic_slice_in_dim(table, first_comp, row_count, axis=1)
    return jnp.pad(own, ((0, 4), (0, -row_count % LANES)))


def cuts_of(row_count):
    middle = row_count // 2 // 16 * 16
    return [(0, middle), (middle, row_count)]


def shards(
    spectrum,
    wave_speed,
    current_east,
    current_north,
    substeps,
    neighbours,
    blocks,
    quad_index,
    strength,
):
    peers = lax.axis_size("comp")
    row_count, columns = spectrum.shape
    own_index = lax.axis_index("comp").astype(jnp.int32)
    turn = own_index.reshape(1)
    odd = lax.rem(lax.axis_index("space").astype(jnp.int32), 2).reshape(1)
    rows = row_table(own_index * row_count, row_count, substeps, wave_speed)
    turned = blocks.swapaxes(1, 2)
    if columns == DEEP and peers == TILES and row_count % 16 == 0:
        cuts = cuts_of(row_count)
        sent = [[] for _ in range(peers)]
        tables, moved = None, None
        for low, high in cuts:
            if tables is None:
                chunk = pack(neighbours, current_east, current_north, spectrum, high)
            else:
                chunk, near = lax.optimization_barrier((spectrum[low:high], tables[0]))
                tables = (near, *tables[1:])
            sides = from_pairs(chunk)
            first = 0 if tables else 8
            tables = tables or sides
            moved = propagate(turn, odd, rows, tables, sides, first, low, high - low)
            for m in range(peers):
                piece = moved[m]
                if m:
                    piece = lax.ppermute(piece, "comp", [(i, (i + m) % peers) for i in range(peers)])
                sent[m].append(piece)
        pieces = [piece for group in sent for piece in group]
        starts = [[low for low, high in cuts]] * peers
        results = source_term(turn, pieces, starts, quad_index, strength, blocks, turned, peers)
        back = [
            lax.ppermute(piece, "comp", [(i, (i + m) % peers) for i in range(peers)]) if m else piece
            for m, piece in enumerate(results)
        ]
        return gather_columns(turn, back)
    still = jnp.zeros((1,), jnp.int32)
    extra = -row_count % 16
    chunk = jnp.pad(spectrum, ((0, extra), (0, 0)))
    before, after = from_sides(chunk, DEEP)
    wide = jnp.concatenate([before, chunk, after], axis=1)
    table = point_table(neighbours, current_east, current_north)
    before, after = from_sides(table, DEEP)
    table = jnp.concatenate([before, table, after], axis=1)
    tiles = []
    for start in range(0, columns, DEEP):
        sides = [wide[:, start + j * DEEP : start + (j + 1) * DEEP] for j in range(3)]
        tables = [table[:, start + j * DEEP : start + (j + 1) * DEEP] for j in range(3)]
        tiles += propagate(still, still + 1, rows, tables, sides, 0, 0, row_count + extra)
    grid = jnp.concatenate(tiles, axis=1)[:row_count].reshape(row_count, peers, columns // peers).swapaxes(0, 1)
    arrived = lax.all_to_all(grid, "comp", 0, 0, tiled=True)
    arrived = arrived.reshape(NF * ND, columns // peers)
    (results,) = source_term(still, [arrived], [[0]], quad_index, strength, blocks, turned, 1)
    results = results.reshape(peers, row_count, columns // peers)
    back = lax.all_to_all(results, "comp", 0, 0, tiled=True)
    return back.swapaxes(0, 1).reshape(row_count, columns)


def solution(mesh):
    in_specs = (
        P("comp", ("grp", "space")),
        P(),
        P(("grp", "space")),
        P(("grp", "space")),
        P(),
        P(None, ("grp", "space")),
        P(),
        P(),
        P(),
    )
    out_specs = P("comp", ("grp", "space"))
    return jax.shard_map(shards, mesh=mesh, in_specs=in_specs, out_specs=out_specs, check_vma=False)
```

```python
import functools
import math

import jax
import jax.numpy as jnp
from jax import lax
from jax.experimental import pallas as pl
from jax.experimental.pallas import tpu as pltpu
from jax.sharding import PartitionSpec as P

NF = 36
ND = 64
SUB = 4
HALO = 128
DEEP = SUB * HALO
LANES = 128
TILES = DEEP // LANES

courant_scale = 0.4
courant_limit = 0.45
source_step = 0.1

VMEM = pl.BlockSpec(memory_space=pltpu.VMEM)
SMEM = pl.BlockSpec(memory_space=pltpu.SMEM)
PARAMS = pltpu.CompilerParams(vmem_limit_bytes=24 << 20)


def in_vmem(values):
    return pltpu.with_memory_space_constraint(values, pltpu.VMEM)


def in_hbm(values):
    return pltpu.with_memory_space_constraint(values, pltpu.HBM)


def split(values):
    high = values.astype(jnp.bfloat16)
    return high, (values - high.astype(jnp.float32)).astype(jnp.bfloat16)


def lane_tile(t, width=1):
    if isinstance(t, int):
        return slice(t * LANES, (t + width) * LANES)
    return pl.ds(pl.multiple_of(t * LANES, LANES), width * LANES)


def propagate_kernel(first, low, turn, odd, rows, *refs):
    table, sides, outs = refs[0], refs[1:4], refs[4 : 4 + TILES]
    field, parts_a, parts_b, along_x, along_y, behind_pick, ahead_pick = refs[-7:]
    parts = (parts_a, parts_b)
    count = field.shape[0]
    total = 3 * TILES
    turned = odd[0] == 1
    columns = jnp.transpose(rows[...])[low : low + count]
    east, north, inverse, substeps = (jnp.broadcast_to(columns[:, c : c + 1], (count, LANES)) for c in range(4))
    position = lax.broadcasted_iota(jnp.int32, (2 * LANES, LANES), 0).astype(jnp.float32)

    def region(group, taken, t):
        cols = lane_tile(t % TILES)
        near, own, far = (ref[taken, cols] for ref in group)
        if t < TILES:
            return jnp.where(turned, near, far)
        return own if t < 2 * TILES else jnp.where(turned, far, near)

    def prepare(t):
        values = region(sides, slice(first, first + count), t)
        field[:, lane_tile(t)] = values
        parts_a[:count, lane_tile(t)], parts_a[count:, lane_tile(t)] = split(values)
        if 0 < t < total - 1:
            near_table = table[:, lane_tile(t)]
            for pick, side in ((behind_pick, 0), (ahead_pick, 1)):
                for d in range(2):
                    chosen = position == near_table[2 * d + side : 2 * d + side + 1]
                    pick[t, :, lane_tile(d)] = jnp.where(chosen, 1.0, 0.0).astype(jnp.bfloat16)
            limit = near_table[6:7]
            along_x[t] = jnp.clip(east + inverse * near_table[4:5], -limit, limit)
            along_y[t] = jnp.clip(north + inverse * near_table[5:6], -limit, limit)

    if first:
        table = refs[4 + TILES]
        for t in range(total):
            table[:, lane_tile(t)] = region(sides, slice(0, 8), t)
    prepare(0)
    prepare(1)
    for s in range(SUB):
        source, target = parts[s % 2], parts[1 - s % 2]
        for t in range(s + 1, total - 1 - s):
            cols = lane_tile(t)
            if s == 0:
                prepare(t + 1)
            behind = jnp.dot(source[:, lane_tile(t - 1, 2)], behind_pick[t], preferred_element_type=jnp.float32)
            ahead = jnp.dot(source[:, lane_tile(t, 2)], ahead_pick[t], preferred_element_type=jnp.float32)
            behind = behind[:count] + behind[count:]
            ahead = ahead[:count] + ahead[count:]
            values = field[:, cols]
            updated = values
            for d, along in enumerate((along_x, along_y)):
                speed = along[t]
                upwind = jnp.where(speed > 0, behind[:, lane_tile(d)], ahead[:, lane_tile(d)])
                updated = updated - jnp.abs(speed) * (values - upwind)
            if s:
                updated = jnp.where(substeps > s, updated, values)
            field[:, cols] = updated
            if s < SUB - 1:
                target[:count, cols], target[count:, cols] = split(updated)
    for m, out in enumerate(outs):
        out[...] = field[:, lane_tile(lax.rem(turn[0] + m, TILES) + TILES)]


def propagate(turn, odd, rows, table, sides, first, low, count):
    total = 3 * TILES
    shapes = [(count, LANES)] * (TILES - 1) + [(8, 3 * DEEP)] * (first > 0)
    return pl.pallas_call(
        functools.partial(propagate_kernel, first, low),
        out_shape=[pltpu.HBM((count, LANES), jnp.float32)] + [pltpu.VMEM(shape, jnp.float32) for shape in shapes],
        in_specs=[SMEM] * 2 + [VMEM] * 5,
        out_specs=[VMEM] * (1 + len(shapes)),
        scratch_shapes=[
            pltpu.VMEM((count, 3 * DEEP), jnp.float32),
            pltpu.VMEM((2 * count, 3 * DEEP), jnp.bfloat16),
            pltpu.VMEM((2 * count, 3 * DEEP), jnp.bfloat16),
            pltpu.VMEM((total, count, LANES), jnp.float32),
            pltpu.VMEM((total, count, LANES), jnp.float32),
            pltpu.VMEM((total, 2 * LANES, 2 * LANES), jnp.bfloat16),
            pltpu.VMEM((total, 2 * LANES, 2 * LANES), jnp.bfloat16),
        ],
        compiler_params=PARAMS,
        name="propagate",
    )(turn, odd, *map(in_vmem, (rows, table, *sides)))


def source_kernel(starts, step, arrived, quad, strength, turn, blocks, turned, *refs):
    ins, outs, (field, rounded, total) = refs[:arrived], refs[arrived:-3], refs[-3:]
    peers = len(outs)
    row_count = field.shape[0] // peers
    for m, group in enumerate(starts):
        base = lax.rem(turn[0] + peers - m, peers) * row_count
        for offset, ref in zip(group, ins[m * len(group) : (m + 1) * len(group)]):
            rows = pl.ds(pl.multiple_of(base + offset, 16), ref.shape[0])
            values = ref[...]
            field[rows, :] = values
            total[rows, :] = values
            rounded[rows, :] = values.astype(jnp.bfloat16)

    def rows_of(f):
        return pl.ds(pl.multiple_of(f * ND, ND), ND)

    def some(g, carry):
        products = []
        for k in range(step):
            j = g * step + k
            left = jnp.dot(blocks[j], rounded[rows_of(quad[0, j]), :], preferred_element_type=jnp.float32)
            right = jnp.dot(turned[j], rounded[rows_of(quad[1, j]), :], preferred_element_type=jnp.float32)
            products.append((left * right * field[rows_of(quad[2, j]), :]).astype(jnp.bfloat16))
        for k in range(step):
            j = g * step + k
            part = jnp.dot(blocks[j], products[k], preferred_element_type=jnp.float32)
            rows = rows_of(quad[3, j])
            total[rows, :] += (source_step * strength[j]) * part
        return carry

    lax.fori_loop(0, blocks.shape[0] // step, some, 0)
    for m, out in enumerate(outs):
        base = lax.rem(turn[0] + m, peers) * row_count
        out[...] = total[pl.ds(pl.multiple_of(base, 8), row_count), :]


def source_term(turn, pieces, starts, quad_index, strength, blocks, turned, peers):
    columns = pieces[0].shape[1]
    row_count = NF * ND // peers
    step = math.gcd(blocks.shape[0], 16)
    return pl.pallas_call(
        functools.partial(source_kernel, starts, step, len(pieces)),
        out_shape=[pltpu.VMEM((row_count, columns), jnp.float32)] * peers,
        in_specs=[SMEM] * 3 + [VMEM] * (2 + len(pieces)),
        out_specs=[VMEM] * peers,
        scratch_shapes=[
            pltpu.VMEM((NF * ND, columns), jnp.float32),
            pltpu.VMEM((NF * ND, columns), jnp.bfloat16),
            pltpu.VMEM((NF * ND, columns), jnp.float32),
        ],
        compiler_params=PARAMS,
        name="source",
    )(quad_index, strength, turn, in_vmem(blocks), in_vmem(turned), *map(in_vmem, pieces))


def gather_kernel(turn, *refs):
    ins, out = refs[:-1], refs[-1]
    peers = len(ins)
    for m, ref in enumerate(ins):
        out[:, lane_tile(lax.rem(turn[0] + peers - m, peers))] = ref[...]


def gather_columns(turn, pieces):
    rows, columns = pieces[0].shape
    return pl.pallas_call(
        gather_kernel,
        out_shape=jax.ShapeDtypeStruct((rows, columns * len(pieces)), jnp.float32),
        in_specs=[SMEM] + [VMEM] * len(pieces),
        out_specs=VMEM,
        compiler_params=PARAMS,
        name="columns",
    )(turn, *map(in_vmem, pieces))


def from_sides(cells, width):
    count = lax.axis_size("space")
    head, tail = cells[:, :width], cells[:, cells.shape[1] - width :]
    before = lax.ppermute(tail, "space", [(i, i + 1) for i in range(count - 1)])
    after = lax.ppermute(head, "space", [(i + 1, i) for i in range(count - 1)])
    return before, after


def from_pairs(cells):
    count = lax.axis_size("space")
    pairs = [[], []]
    for i in range(count - 1):
        pairs[i % 2] += [(i, i + 1), (i + 1, i)]
    far = lax.ppermute(cells, "space", pairs[1])
    near = lax.ppermute(cells, "space", pairs[0])
    return near, cells, far


def point_table(neighbours, current_east, current_north):
    columns = neighbours.shape[1]
    tile = jnp.arange(columns, dtype=jnp.int32) // LANES * LANES
    west, east, south, north = neighbours
    return jnp.stack(
        [
            (west - tile).astype(jnp.float32),
            (east - tile - LANES).astype(jnp.float32),
            (south - tile).astype(jnp.float32),
            (north - tile - LANES).astype(jnp.float32),
            current_east,
            current_north,
            jnp.full((columns,), courant_limit, jnp.float32),
            jnp.zeros((columns,), jnp.float32),
        ]
    )


def pack_kernel(neighbours, east, north, cells, out):
    columns = out.shape[1]
    tile = lax.broadcasted_iota(jnp.int32, (4, columns), 1) // LANES * LANES
    ahead = lax.broadcasted_iota(jnp.int32, (4, columns), 0) % 2 * LANES
    out[0:4] = (neighbours[...] - tile - ahead).astype(jnp.float32)
    out[4:5] = east[...].reshape(1, columns)
    out[5:6] = north[...].reshape(1, columns)
    out[6:8] = jnp.full((2, columns), courant_limit, jnp.float32)
    out[8:] = cells[...]


def pack(neighbours, east, north, spectrum, count):
    columns = spectrum.shape[1]
    return pl.pallas_call(
        pack_kernel,
        grid=(1,),
        out_shape=pltpu.VMEM((8 + count, columns), jnp.float32),
        in_specs=[
            pl.BlockSpec((4, columns), lambda i: (0, 0)),
            pl.BlockSpec((1, columns), lambda i: (0, 0)),
            pl.BlockSpec((1, columns), lambda i: (0, 0)),
            pl.BlockSpec((count, columns), lambda i: (0, 0)),
        ],
        out_specs=pl.BlockSpec((8 + count, columns), lambda i: (0, 0)),
        compiler_params=PARAMS,
        name="pack",
    )(*map(in_hbm, (neighbours, east[None], north[None], spectrum)))


def rows_kernel(low, cells, out, flag):
    copy = pltpu.make_async_copy(cells.at[low : low + out.shape[0], :], out, flag)
    copy.start()
    copy.wait()


def rows_from(spectrum, low, high):
    return pl.pallas_call(
        functools.partial(rows_kernel, low),
        out_shape=pltpu.VMEM((high - low, spectrum.shape[1]), jnp.float32),
        in_specs=[pl.BlockSpec(memory_space=pl.ANY)],
        out_specs=VMEM,
        scratch_shapes=[pltpu.SemaphoreType.DMA],
        compiler_params=PARAMS,
        name="rest",
    )(in_hbm(spectrum))


def row_table(first_comp, row_count, substeps, wave_speed):
    angles = (jnp.arange(ND, dtype=jnp.float32) + 0.5) * (2.0 * math.pi / ND)
    inverse = courant_scale / substeps.astype(jnp.float32)
    speed = wave_speed[:, None]
    along = [(speed * wave(angles)[None, :]).reshape(NF * ND) * inverse for wave in (jnp.cos, jnp.sin)]
    table = jnp.stack(along + [inverse, substeps.astype(jnp.float32)])
    own = lax.dynamic_slice_in_dim(table, first_comp, row_count, axis=1)
    return jnp.pad(own, ((0, 4), (0, -row_count % LANES)))


def cuts_of(row_count):
    middle = row_count * 5 // 8 // 32 * 32
    return [(0, middle), (middle, row_count)]


def shards(
    spectrum,
    wave_speed,
    current_east,
    current_north,
    substeps,
    neighbours,
    blocks,
    quad_index,
    strength,
):
    peers = lax.axis_size("comp")
    row_count, columns = spectrum.shape
    own_index = lax.axis_index("comp").astype(jnp.int32)
    turn = own_index.reshape(1)
    odd = lax.rem(lax.axis_index("space").astype(jnp.int32), 2).reshape(1)
    rows = row_table(own_index * row_count, row_count, substeps, wave_speed)
    turned = blocks.swapaxes(1, 2)
    if columns == DEEP and peers == TILES and row_count % 16 == 0:
        cuts = cuts_of(row_count)
        sent = [[] for _ in range(peers)]
        chunk = pack(neighbours, current_east, current_north, spectrum, cuts[0][1])
        sides, table = from_pairs(chunk), rows
        for low, high in cuts:
            first = 0 if low else 8
            coming = None
            if high < row_count:
                chunk, near = lax.optimization_barrier((rows_from(spectrum, high, row_count), sides[0]))
                sides = (near, *sides[1:])
                coming = from_pairs(chunk)
            moved = propagate(turn, odd, rows, table, sides, first, low, high - low)
            sides, table = coming, moved[-1]
            for m in range(peers):
                piece = moved[m]
                if m:
                    piece = lax.ppermute(piece, "comp", [(i, (i + m) % peers) for i in range(peers)])
                sent[m].append(piece)
        pieces = [piece for group in sent for piece in group]
        starts = [[low for low, high in cuts]] * peers
        results = source_term(turn, pieces, starts, quad_index, strength, blocks, turned, peers)
        back = [
            lax.ppermute(piece, "comp", [(i, (i + m) % peers) for i in range(peers)]) if m else piece
            for m, piece in enumerate(results)
        ]
        return gather_columns(turn, back)
    still = jnp.zeros((1,), jnp.int32)
    extra = -row_count % 16
    chunk = jnp.pad(spectrum, ((0, extra), (0, 0)))
    before, after = from_sides(chunk, DEEP)
    wide = jnp.concatenate([before, chunk, after], axis=1)
    table = point_table(neighbours, current_east, current_north)
    before, after = from_sides(table, DEEP)
    table = jnp.concatenate([before, table, after], axis=1)
    tiles = []
    for start in range(0, columns, DEEP):
        sides = [wide[:, start + j * DEEP : start + (j + 1) * DEEP] for j in range(3)]
        near = table[:, start : start + 3 * DEEP]
        tiles += propagate(still, still + 1, rows, near, sides, 0, 0, row_count + extra)
    grid = jnp.concatenate(tiles, axis=1)[:row_count].reshape(row_count, peers, columns // peers).swapaxes(0, 1)
    arrived = lax.all_to_all(grid, "comp", 0, 0, tiled=True)
    arrived = arrived.reshape(NF * ND, columns // peers)
    (results,) = source_term(still, [arrived], [[0]], quad_index, strength, blocks, turned, 1)
    results = results.reshape(peers, row_count, columns // peers)
    back = lax.all_to_all(results, "comp", 0, 0, tiled=True)
    return back.swapaxes(0, 1).reshape(row_count, columns)


def solution(mesh):
    in_specs = (
        P("comp", ("grp", "space")),
        P(),
        P(("grp", "space")),
        P(("grp", "space")),
        P(),
        P(None, ("grp", "space")),
        P(),
        P(),
        P(),
    )
    out_specs = P("comp", ("grp", "space"))
    return jax.shard_map(shards, mesh=mesh, in_specs=in_specs, out_specs=out_specs, check_vma=False)
```

```python
import functools
import math

import jax
import jax.numpy as jnp
from jax import lax
from jax.experimental import pallas as pl
from jax.experimental.pallas import tpu as pltpu
from jax.sharding import PartitionSpec as P

NF = 36
ND = 64
SUB = 4
HALO = 128
DEEP = SUB * HALO
LANES = 128
TILES = DEEP // LANES

courant_scale = 0.4
courant_limit = 0.45
source_step = 0.1

VMEM = pl.BlockSpec(memory_space=pltpu.VMEM)
SMEM = pl.BlockSpec(memory_space=pltpu.SMEM)
PARAMS = pltpu.CompilerParams(vmem_limit_bytes=24 << 20)


def in_vmem(values):
    return pltpu.with_memory_space_constraint(values, pltpu.VMEM)


def in_hbm(values):
    return pltpu.with_memory_space_constraint(values, pltpu.HBM)


def split(values):
    high = values.astype(jnp.bfloat16)
    return high, (values - high.astype(jnp.float32)).astype(jnp.bfloat16)


def lane_tile(t, width=1):
    if isinstance(t, int):
        return slice(t * LANES, (t + width) * LANES)
    return pl.ds(pl.multiple_of(t * LANES, LANES), width * LANES)


def propagate_kernel(first, low, turn, odd, rows, *refs):
    table, sides, outs = refs[0], refs[1:4], refs[4 : 4 + TILES]
    field, parts_a, parts_b, along_x, along_y, behind_pick, ahead_pick = refs[-7:]
    parts = (parts_a, parts_b)
    count = field.shape[0]
    total = 3 * TILES
    turned = odd[0] == 1
    columns = jnp.transpose(rows[...])[low : low + count]
    east, north, inverse, substeps = (jnp.broadcast_to(columns[:, c : c + 1], (count, LANES)) for c in range(4))
    position = lax.broadcasted_iota(jnp.int32, (2 * LANES, LANES), 0).astype(jnp.float32)

    def region(group, taken, t):
        cols = lane_tile(t % TILES)
        near, own, far = (ref[taken, cols] for ref in group)
        if t < TILES:
            return jnp.where(turned, near, far)
        return own if t < 2 * TILES else jnp.where(turned, far, near)

    def prepare(t):
        values = region(sides, slice(first, first + count), t)
        field[:, lane_tile(t)] = values
        parts_a[:count, lane_tile(t)], parts_a[count:, lane_tile(t)] = split(values)
        if 0 < t < total - 1:
            near_table = table[:, lane_tile(t)]
            for pick, side in ((behind_pick, 0), (ahead_pick, 1)):
                for d in range(2):
                    chosen = position == near_table[2 * d + side : 2 * d + side + 1]
                    pick[t, :, lane_tile(d)] = jnp.where(chosen, 1.0, 0.0).astype(jnp.bfloat16)
            limit = near_table[6:7]
            along_x[t] = jnp.clip(east + inverse * near_table[4:5], -limit, limit)
            along_y[t] = jnp.clip(north + inverse * near_table[5:6], -limit, limit)

    if first:
        table = refs[4 + TILES]
        for t in range(total):
            table[:, lane_tile(t)] = region(sides, slice(0, 8), t)
    prepare(0)
    prepare(1)
    for s in range(SUB):
        source, target = parts[s % 2], parts[1 - s % 2]
        for t in range(s + 1, total - 1 - s):
            cols = lane_tile(t)
            if s == 0:
                prepare(t + 1)
            behind = jnp.dot(source[:, lane_tile(t - 1, 2)], behind_pick[t], preferred_element_type=jnp.float32)
            ahead = jnp.dot(source[:, lane_tile(t, 2)], ahead_pick[t], preferred_element_type=jnp.float32)
            behind = behind[:count] + behind[count:]
            ahead = ahead[:count] + ahead[count:]
            values = field[:, cols]
            updated = values
            for d, along in enumerate((along_x, along_y)):
                speed = along[t]
                upwind = jnp.where(speed > 0, behind[:, lane_tile(d)], ahead[:, lane_tile(d)])
                updated = updated - jnp.abs(speed) * (values - upwind)
            if s:
                updated = jnp.where(substeps > s, updated, values)
            field[:, cols] = updated
            if s < SUB - 1:
                target[:count, cols], target[count:, cols] = split(updated)
    for m, out in enumerate(outs):
        out[...] = field[:, lane_tile(lax.rem(turn[0] + m, TILES) + TILES)]


def propagate(turn, odd, rows, table, sides, first, low, count):
    total = 3 * TILES
    shapes = [(count, LANES)] * (TILES - 1) + [(8, 3 * DEEP)] * (first > 0)
    return pl.pallas_call(
        functools.partial(propagate_kernel, first, low),
        out_shape=[pltpu.HBM((count, LANES), jnp.float32)] + [pltpu.VMEM(shape, jnp.float32) for shape in shapes],
        in_specs=[SMEM] * 2 + [VMEM] * 5,
        out_specs=[VMEM] * (1 + len(shapes)),
        scratch_shapes=[
            pltpu.VMEM((count, 3 * DEEP), jnp.float32),
            pltpu.VMEM((2 * count, 3 * DEEP), jnp.bfloat16),
            pltpu.VMEM((2 * count, 3 * DEEP), jnp.bfloat16),
            pltpu.VMEM((total, count, LANES), jnp.float32),
            pltpu.VMEM((total, count, LANES), jnp.float32),
            pltpu.VMEM((total, 2 * LANES, 2 * LANES), jnp.bfloat16),
            pltpu.VMEM((total, 2 * LANES, 2 * LANES), jnp.bfloat16),
        ],
        compiler_params=PARAMS,
        name="propagate",
    )(turn, odd, *map(in_vmem, (rows, table, *sides)))


def source_kernel(starts, step, arrived, quad, strength, turn, blocks, turned, *refs):
    ins, outs, (field, rounded, total) = refs[:arrived], refs[arrived:-3], refs[-3:]
    peers = len(outs)
    row_count = field.shape[0] // peers
    for m, group in enumerate(starts):
        base = lax.rem(turn[0] + peers - m, peers) * row_count
        for offset, ref in zip(group, ins[m * len(group) : (m + 1) * len(group)]):
            rows = pl.ds(pl.multiple_of(base + offset, 16), ref.shape[0])
            values = ref[...]
            field[rows, :] = values
            total[rows, :] = values
            rounded[rows, :] = values.astype(jnp.bfloat16)

    def rows_of(f):
        return pl.ds(pl.multiple_of(f * ND, ND), ND)

    def some(g, carry):
        products = []
        for k in range(step):
            j = g * step + k
            left = jnp.dot(blocks[j], rounded[rows_of(quad[0, j]), :], preferred_element_type=jnp.float32)
            right = jnp.dot(turned[j], rounded[rows_of(quad[1, j]), :], preferred_element_type=jnp.float32)
            products.append((left * right * field[rows_of(quad[2, j]), :]).astype(jnp.bfloat16))
        for k in range(step):
            j = g * step + k
            part = jnp.dot(blocks[j], products[k], preferred_element_type=jnp.float32)
            rows = rows_of(quad[3, j])
            total[rows, :] += (source_step * strength[j]) * part
        return carry

    lax.fori_loop(0, blocks.shape[0] // step, some, 0)
    for m, out in enumerate(outs):
        base = lax.rem(turn[0] + m, peers) * row_count
        out[...] = total[pl.ds(pl.multiple_of(base, 8), row_count), :]


def source_term(turn, pieces, starts, quad_index, strength, blocks, turned, peers):
    columns = pieces[0].shape[1]
    row_count = NF * ND // peers
    step = math.gcd(blocks.shape[0], 16)
    return pl.pallas_call(
        functools.partial(source_kernel, starts, step, len(pieces)),
        out_shape=[pltpu.VMEM((row_count, columns), jnp.float32)] * peers,
        in_specs=[SMEM] * 3 + [VMEM] * (2 + len(pieces)),
        out_specs=[VMEM] * peers,
        scratch_shapes=[
            pltpu.VMEM((NF * ND, columns), jnp.float32),
            pltpu.VMEM((NF * ND, columns), jnp.bfloat16),
            pltpu.VMEM((NF * ND, columns), jnp.float32),
        ],
        compiler_params=PARAMS,
        name="source",
    )(quad_index, strength, turn, in_vmem(blocks), in_vmem(turned), *map(in_vmem, pieces))


def gather_kernel(turn, *refs):
    ins, out = refs[:-1], refs[-1]
    peers = len(ins)
    for m, ref in enumerate(ins):
        out[:, lane_tile(lax.rem(turn[0] + peers - m, peers))] = ref[...]


def gather_columns(turn, pieces):
    rows, columns = pieces[0].shape
    return pl.pallas_call(
        gather_kernel,
        out_shape=jax.ShapeDtypeStruct((rows, columns * len(pieces)), jnp.float32),
        in_specs=[SMEM] + [VMEM] * len(pieces),
        out_specs=VMEM,
        compiler_params=PARAMS,
        name="columns",
    )(turn, *map(in_vmem, pieces))


def from_sides(cells, width):
    count = lax.axis_size("space")
    head, tail = cells[:, :width], cells[:, cells.shape[1] - width :]
    before = lax.ppermute(tail, "space", [(i, i + 1) for i in range(count - 1)])
    after = lax.ppermute(head, "space", [(i + 1, i) for i in range(count - 1)])
    return before, after


def from_pairs(cells, gate=None):
    count = lax.axis_size("space")
    pairs = [[], []]
    for i in range(count - 1):
        pairs[i % 2] += [(i, i + 1), (i + 1, i)]
    near = lax.ppermute(cells, "space", pairs[0])
    held = cells
    if gate is not None:
        held, gate = lax.optimization_barrier((cells, gate))
    far = lax.ppermute(held, "space", pairs[1])
    return (near, cells, far), gate


def point_table(neighbours, current_east, current_north):
    columns = neighbours.shape[1]
    tile = jnp.arange(columns, dtype=jnp.int32) // LANES * LANES
    west, east, south, north = neighbours
    return jnp.stack(
        [
            (west - tile).astype(jnp.float32),
            (east - tile - LANES).astype(jnp.float32),
            (south - tile).astype(jnp.float32),
            (north - tile - LANES).astype(jnp.float32),
            current_east,
            current_north,
            jnp.full((columns,), courant_limit, jnp.float32),
            jnp.zeros((columns,), jnp.float32),
        ]
    )


def pack_kernel(neighbours, east, north, cells, out):
    columns = out.shape[1]
    tile = lax.broadcasted_iota(jnp.int32, (4, columns), 1) // LANES * LANES
    ahead = lax.broadcasted_iota(jnp.int32, (4, columns), 0) % 2 * LANES
    out[0:4] = (neighbours[...] - tile - ahead).astype(jnp.float32)
    out[4:5] = east[...].reshape(1, columns)
    out[5:6] = north[...].reshape(1, columns)
    out[6:8] = jnp.full((2, columns), courant_limit, jnp.float32)
    out[8:] = cells[...]


def pack(neighbours, east, north, spectrum, count):
    columns = spectrum.shape[1]
    return pl.pallas_call(
        pack_kernel,
        grid=(1,),
        out_shape=pltpu.VMEM((8 + count, columns), jnp.float32),
        in_specs=[
            pl.BlockSpec((4, columns), lambda i: (0, 0)),
            pl.BlockSpec((1, columns), lambda i: (0, 0)),
            pl.BlockSpec((1, columns), lambda i: (0, 0)),
            pl.BlockSpec((count, columns), lambda i: (0, 0)),
        ],
        out_specs=pl.BlockSpec((8 + count, columns), lambda i: (0, 0)),
        compiler_params=PARAMS,
        name="pack",
    )(*map(in_hbm, (neighbours, east[None], north[None], spectrum)))


def row_table(first_comp, row_count, substeps, wave_speed):
    angles = (jnp.arange(ND, dtype=jnp.float32) + 0.5) * (2.0 * math.pi / ND)
    inverse = courant_scale / substeps.astype(jnp.float32)
    speed = wave_speed[:, None]
    along = [(speed * wave(angles)[None, :]).reshape(NF * ND) * inverse for wave in (jnp.cos, jnp.sin)]
    table = jnp.stack(along + [inverse, substeps.astype(jnp.float32)])
    own = lax.dynamic_slice_in_dim(table, first_comp, row_count, axis=1)
    return jnp.pad(own, ((0, 4), (0, -row_count % LANES)))


def cuts_of(row_count):
    middle = row_count // 2 // 16 * 16
    return [(0, middle), (middle, row_count)]


def shards(
    spectrum,
    wave_speed,
    current_east,
    current_north,
    substeps,
    neighbours,
    blocks,
    quad_index,
    strength,
):
    peers = lax.axis_size("comp")
    row_count, columns = spectrum.shape
    own_index = lax.axis_index("comp").astype(jnp.int32)
    turn = own_index.reshape(1)
    odd = lax.rem(lax.axis_index("space").astype(jnp.int32), 2).reshape(1)
    rows = row_table(own_index * row_count, row_count, substeps, wave_speed)
    turned = blocks.swapaxes(1, 2)
    if columns == DEEP and peers == TILES and row_count % 16 == 0:
        cuts = cuts_of(row_count)
        sent = [[] for _ in range(peers)]
        chunk = pack(neighbours, current_east, current_north, spectrum, cuts[0][1])
        (sides, gate), table = from_pairs(chunk), rows
        for low, high in cuts:
            first = 0 if low else 8
            coming = None
            if high < row_count:
                coming, near = from_pairs(spectrum[high:], sides[0])
                sides = (near, *sides[1:])
            moved = propagate(turn, odd, rows, table, sides, first, low, high - low)
            sides, table = coming, moved[-1]
            for m in range(peers):
                piece = moved[m]
                if m:
                    piece = lax.ppermute(piece, "comp", [(i, (i + m) % peers) for i in range(peers)])
                sent[m].append(piece)
        pieces = [piece for group in sent for piece in group]
        starts = [[low for low, high in cuts]] * peers
        results = source_term(turn, pieces, starts, quad_index, strength, blocks, turned, peers)
        back = [
            lax.ppermute(piece, "comp", [(i, (i + m) % peers) for i in range(peers)]) if m else piece
            for m, piece in enumerate(results)
        ]
        return gather_columns(turn, back)
    still = jnp.zeros((1,), jnp.int32)
    extra = -row_count % 16
    chunk = jnp.pad(spectrum, ((0, extra), (0, 0)))
    before, after = from_sides(chunk, DEEP)
    wide = jnp.concatenate([before, chunk, after], axis=1)
    table = point_table(neighbours, current_east, current_north)
    before, after = from_sides(table, DEEP)
    table = jnp.concatenate([before, table, after], axis=1)
    tiles = []
    for start in range(0, columns, DEEP):
        sides = [wide[:, start + j * DEEP : start + (j + 1) * DEEP] for j in range(3)]
        near = table[:, start : start + 3 * DEEP]
        tiles += propagate(still, still + 1, rows, near, sides, 0, 0, row_count + extra)
    grid = jnp.concatenate(tiles, axis=1)[:row_count].reshape(row_count, peers, columns // peers).swapaxes(0, 1)
    arrived = lax.all_to_all(grid, "comp", 0, 0, tiled=True)
    arrived = arrived.reshape(NF * ND, columns // peers)
    (results,) = source_term(still, [arrived], [[0]], quad_index, strength, blocks, turned, 1)
    results = results.reshape(peers, row_count, columns // peers)
    back = lax.all_to_all(results, "comp", 0, 0, tiled=True)
    return back.swapaxes(0, 1).reshape(row_count, columns)


def solution(mesh):
    in_specs = (
        P("comp", ("grp", "space")),
        P(),
        P(("grp", "space")),
        P(("grp", "space")),
        P(),
        P(None, ("grp", "space")),
        P(),
        P(),
        P(),
    )
    out_specs = P("comp", ("grp", "space"))
    return jax.shard_map(shards, mesh=mesh, in_specs=in_specs, out_specs=out_specs, check_vma=False)
```

```python
import functools
import math

import jax
import jax.numpy as jnp
from jax import lax
from jax.experimental import pallas as pl
from jax.experimental.pallas import tpu as pltpu
from jax.sharding import PartitionSpec as P

NF = 36
ND = 64
SUB = 4
HALO = 128
DEEP = SUB * HALO
LANES = 128
TILES = DEEP // LANES

courant_scale = 0.4
courant_limit = 0.45
source_step = 0.1

VMEM = pl.BlockSpec(memory_space=pltpu.VMEM)
SMEM = pl.BlockSpec(memory_space=pltpu.SMEM)
PARAMS = pltpu.CompilerParams(vmem_limit_bytes=24 << 20)


def in_vmem(values):
    return pltpu.with_memory_space_constraint(values, pltpu.VMEM)


def in_hbm(values):
    return pltpu.with_memory_space_constraint(values, pltpu.HBM)


def split(values):
    high = values.astype(jnp.bfloat16)
    return high, (values - high.astype(jnp.float32)).astype(jnp.bfloat16)


def lane_tile(t, width=1):
    if isinstance(t, int):
        return slice(t * LANES, (t + width) * LANES)
    return pl.ds(pl.multiple_of(t * LANES, LANES), width * LANES)


def propagate_kernel(first, low, turn, odd, rows, *refs):
    table, sides, outs = refs[0], refs[1:4], refs[4 : 4 + TILES]
    field, parts_a, parts_b, along_x, along_y, behind_pick, ahead_pick = refs[-7:]
    parts = (parts_a, parts_b)
    count = field.shape[0]
    total = 3 * TILES
    turned = odd[0] == 1
    columns = jnp.transpose(rows[...])[low : low + count]
    east, north, inverse, substeps = (jnp.broadcast_to(columns[:, c : c + 1], (count, LANES)) for c in range(4))
    position = lax.broadcasted_iota(jnp.int32, (2 * LANES, LANES), 0).astype(jnp.float32)

    def region(group, taken, t):
        cols = lane_tile(t % TILES)
        near, own, far = (ref[taken, cols] for ref in group)
        if t < TILES:
            return jnp.where(turned, near, far)
        return own if t < 2 * TILES else jnp.where(turned, far, near)

    def prepare(t):
        values = region(sides, slice(first, first + count), t)
        field[:, lane_tile(t)] = values
        parts_a[:count, lane_tile(t)], parts_a[count:, lane_tile(t)] = split(values)
        if 0 < t < total - 1:
            near_table = table[:, lane_tile(t)]
            for pick, side in ((behind_pick, 0), (ahead_pick, 1)):
                for d in range(2):
                    chosen = position == near_table[2 * d + side : 2 * d + side + 1]
                    pick[t, :, lane_tile(d)] = jnp.where(chosen, 1.0, 0.0).astype(jnp.bfloat16)
            limit = near_table[6:7]
            along_x[t] = jnp.clip(east + inverse * near_table[4:5], -limit, limit)
            along_y[t] = jnp.clip(north + inverse * near_table[5:6], -limit, limit)

    if first:
        table = refs[4 + TILES]
        for t in range(total):
            table[:, lane_tile(t)] = region(sides, slice(0, 8), t)
    prepare(0)
    prepare(1)
    for s in range(SUB):
        source, target = parts[s % 2], parts[1 - s % 2]
        for t in range(s + 1, total - 1 - s):
            cols = lane_tile(t)
            if s == 0:
                prepare(t + 1)
            behind = jnp.dot(source[:, lane_tile(t - 1, 2)], behind_pick[t], preferred_element_type=jnp.float32)
            ahead = jnp.dot(source[:, lane_tile(t, 2)], ahead_pick[t], preferred_element_type=jnp.float32)
            behind = behind[:count] + behind[count:]
            ahead = ahead[:count] + ahead[count:]
            values = field[:, cols]
            updated = values
            for d, along in enumerate((along_x, along_y)):
                speed = along[t]
                upwind = jnp.where(speed > 0, behind[:, lane_tile(d)], ahead[:, lane_tile(d)])
                updated = updated - jnp.abs(speed) * (values - upwind)
            if s:
                updated = jnp.where(substeps > s, updated, values)
            field[:, cols] = updated
            if s < SUB - 1:
                target[:count, cols], target[count:, cols] = split(updated)
    for m, out in enumerate(outs):
        out[...] = field[:, lane_tile(lax.rem(turn[0] + m, TILES) + TILES)]


def propagate(turn, odd, rows, table, sides, first, low, count):
    total = 3 * TILES
    shapes = [(count, LANES)] * (TILES - 1) + [(8, 3 * DEEP)] * (first > 0)
    return pl.pallas_call(
        functools.partial(propagate_kernel, first, low),
        out_shape=[pltpu.HBM((count, LANES), jnp.float32)] + [pltpu.VMEM(shape, jnp.float32) for shape in shapes],
        in_specs=[SMEM] * 2 + [VMEM] * 5,
        out_specs=[VMEM] * (1 + len(shapes)),
        scratch_shapes=[
            pltpu.VMEM((count, 3 * DEEP), jnp.float32),
            pltpu.VMEM((2 * count, 3 * DEEP), jnp.bfloat16),
            pltpu.VMEM((2 * count, 3 * DEEP), jnp.bfloat16),
            pltpu.VMEM((total, count, LANES), jnp.float32),
            pltpu.VMEM((total, count, LANES), jnp.float32),
            pltpu.VMEM((total, 2 * LANES, 2 * LANES), jnp.bfloat16),
            pltpu.VMEM((total, 2 * LANES, 2 * LANES), jnp.bfloat16),
        ],
        compiler_params=PARAMS,
        name="propagate",
    )(turn, odd, *map(in_vmem, (rows, table, *sides)))


def source_kernel(starts, step, arrived, quad, strength, turn, blocks, turned, *refs):
    ins, outs, (field, rounded, total) = refs[:arrived], refs[arrived:-3], refs[-3:]
    peers = len(outs)
    row_count = field.shape[0] // peers
    for m, group in enumerate(starts):
        base = lax.rem(turn[0] + peers - m, peers) * row_count
        for offset, ref in zip(group, ins[m * len(group) : (m + 1) * len(group)]):
            rows = pl.ds(pl.multiple_of(base + offset, 16), ref.shape[0])
            values = ref[...]
            field[rows, :] = values
            total[rows, :] = values
            rounded[rows, :] = values.astype(jnp.bfloat16)

    def rows_of(f):
        return pl.ds(pl.multiple_of(f * ND, ND), ND)

    def some(g, carry):
        products = []
        for k in range(step):
            j = g * step + k
            left = jnp.dot(blocks[j], rounded[rows_of(quad[0, j]), :], preferred_element_type=jnp.float32)
            right = jnp.dot(turned[j], rounded[rows_of(quad[1, j]), :], preferred_element_type=jnp.float32)
            products.append((left * right * field[rows_of(quad[2, j]), :]).astype(jnp.bfloat16))
        for k in range(step):
            j = g * step + k
            part = jnp.dot(blocks[j], products[k], preferred_element_type=jnp.float32)
            rows = rows_of(quad[3, j])
            total[rows, :] += (source_step * strength[j]) * part
        return carry

    lax.fori_loop(0, blocks.shape[0] // step, some, 0)
    for m, out in enumerate(outs):
        base = lax.rem(turn[0] + m, peers) * row_count
        out[...] = total[pl.ds(pl.multiple_of(base, 8), row_count), :]


def source_term(turn, pieces, starts, quad_index, strength, blocks, turned, peers):
    columns = pieces[0].shape[1]
    row_count = NF * ND // peers
    step = math.gcd(blocks.shape[0], 16)
    return pl.pallas_call(
        functools.partial(source_kernel, starts, step, len(pieces)),
        out_shape=[pltpu.VMEM((row_count, columns), jnp.float32)] * peers,
        in_specs=[SMEM] * 3 + [VMEM] * (2 + len(pieces)),
        out_specs=[VMEM] * peers,
        scratch_shapes=[
            pltpu.VMEM((NF * ND, columns), jnp.float32),
            pltpu.VMEM((NF * ND, columns), jnp.bfloat16),
            pltpu.VMEM((NF * ND, columns), jnp.float32),
        ],
        compiler_params=PARAMS,
        name="source",
    )(quad_index, strength, turn, in_vmem(blocks), in_vmem(turned), *map(in_vmem, pieces))


def gather_kernel(turn, *refs):
    ins, out = refs[:-1], refs[-1]
    peers = len(ins)
    for m, ref in enumerate(ins):
        out[:, lane_tile(lax.rem(turn[0] + peers - m, peers))] = ref[...]


def gather_columns(turn, pieces):
    rows, columns = pieces[0].shape
    return pl.pallas_call(
        gather_kernel,
        out_shape=jax.ShapeDtypeStruct((rows, columns * len(pieces)), jnp.float32),
        in_specs=[SMEM] + [VMEM] * len(pieces),
        out_specs=VMEM,
        compiler_params=PARAMS,
        name="columns",
    )(turn, *map(in_vmem, pieces))


def from_sides(cells, width):
    count = lax.axis_size("space")
    head, tail = cells[:, :width], cells[:, cells.shape[1] - width :]
    before = lax.ppermute(tail, "space", [(i, i + 1) for i in range(count - 1)])
    after = lax.ppermute(head, "space", [(i + 1, i) for i in range(count - 1)])
    return before, after


def from_pairs(cells, gate=None):
    count = lax.axis_size("space")
    pairs = [[], []]
    for i in range(count - 1):
        pairs[i % 2] += [(i, i + 1), (i + 1, i)]
    near = lax.ppermute(cells, "space", pairs[0])
    held = cells
    if gate is not None:
        held, gate = lax.optimization_barrier((cells, gate))
    far = lax.ppermute(held, "space", pairs[1])
    return (near, cells, far), gate


def point_table(neighbours, current_east, current_north):
    columns = neighbours.shape[1]
    tile = jnp.arange(columns, dtype=jnp.int32) // LANES * LANES
    west, east, south, north = neighbours
    return jnp.stack(
        [
            (west - tile).astype(jnp.float32),
            (east - tile - LANES).astype(jnp.float32),
            (south - tile).astype(jnp.float32),
            (north - tile - LANES).astype(jnp.float32),
            current_east,
            current_north,
            jnp.full((columns,), courant_limit, jnp.float32),
            jnp.zeros((columns,), jnp.float32),
        ]
    )


def pack_kernel(neighbours, east, north, cells, out):
    columns = out.shape[1]
    tile = lax.broadcasted_iota(jnp.int32, (4, columns), 1) // LANES * LANES
    ahead = lax.broadcasted_iota(jnp.int32, (4, columns), 0) % 2 * LANES
    out[0:4] = (neighbours[...] - tile - ahead).astype(jnp.float32)
    out[4:5] = east[...].reshape(1, columns)
    out[5:6] = north[...].reshape(1, columns)
    out[6:8] = jnp.full((2, columns), courant_limit, jnp.float32)
    out[8:] = cells[...]


def pack(neighbours, east, north, spectrum, count):
    columns = spectrum.shape[1]
    return pl.pallas_call(
        pack_kernel,
        grid=(1,),
        out_shape=pltpu.VMEM((8 + count, columns), jnp.float32),
        in_specs=[
            pl.BlockSpec((4, columns), lambda i: (0, 0)),
            pl.BlockSpec((1, columns), lambda i: (0, 0)),
            pl.BlockSpec((1, columns), lambda i: (0, 0)),
            pl.BlockSpec((count, columns), lambda i: (0, 0)),
        ],
        out_specs=pl.BlockSpec((8 + count, columns), lambda i: (0, 0)),
        compiler_params=PARAMS,
        name="pack",
    )(*map(in_hbm, (neighbours, east[None], north[None], spectrum)))


def row_table(first_comp, row_count, substeps, wave_speed):
    angles = (jnp.arange(ND, dtype=jnp.float32) + 0.5) * (2.0 * math.pi / ND)
    inverse = courant_scale / substeps.astype(jnp.float32)
    speed = wave_speed[:, None]
    along = [(speed * wave(angles)[None, :]).reshape(NF * ND) * inverse for wave in (jnp.cos, jnp.sin)]
    table = jnp.stack(along + [inverse, substeps.astype(jnp.float32)])
    own = lax.dynamic_slice_in_dim(table, first_comp, row_count, axis=1)
    return jnp.pad(own, ((0, 4), (0, -row_count % LANES)))


def cuts_of(row_count):
    middle = row_count * 17 // 36 // 16 * 16
    return [(0, middle), (middle, row_count)]


def shards(
    spectrum,
    wave_speed,
    current_east,
    current_north,
    substeps,
    neighbours,
    blocks,
    quad_index,
    strength,
):
    peers = lax.axis_size("comp")
    row_count, columns = spectrum.shape
    own_index = lax.axis_index("comp").astype(jnp.int32)
    turn = own_index.reshape(1)
    odd = lax.rem(lax.axis_index("space").astype(jnp.int32), 2).reshape(1)
    rows = row_table(own_index * row_count, row_count, substeps, wave_speed)
    turned = blocks.swapaxes(1, 2)
    if columns == DEEP and peers == TILES and row_count % 16 == 0:
        cuts = cuts_of(row_count)
        sent = [[] for _ in range(peers)]
        chunk = pack(neighbours, current_east, current_north, spectrum, cuts[0][1])
        (sides, gate), table = from_pairs(chunk), rows
        for low, high in cuts:
            first = 0 if low else 8
            coming = None
            if high < row_count:
                coming, near = from_pairs(spectrum[high:], sides[0])
                sides = (near, *sides[1:])
            moved = propagate(turn, odd, rows, table, sides, first, low, high - low)
            sides, table = coming, moved[-1]
            for m in range(peers):
                piece = moved[m]
                if m:
                    piece = lax.ppermute(piece, "comp", [(i, (i + m) % peers) for i in range(peers)])
                sent[m].append(piece)
        pieces = [piece for group in sent for piece in group]
        starts = [[low for low, high in cuts]] * peers
        results = source_term(turn, pieces, starts, quad_index, strength, blocks, turned, peers)
        back = [
            lax.ppermute(piece, "comp", [(i, (i + m) % peers) for i in range(peers)]) if m else piece
            for m, piece in enumerate(results)
        ]
        return gather_columns(turn, back)
    still = jnp.zeros((1,), jnp.int32)
    extra = -row_count % 16
    chunk = jnp.pad(spectrum, ((0, extra), (0, 0)))
    before, after = from_sides(chunk, DEEP)
    wide = jnp.concatenate([before, chunk, after], axis=1)
    table = point_table(neighbours, current_east, current_north)
    before, after = from_sides(table, DEEP)
    table = jnp.concatenate([before, table, after], axis=1)
    tiles = []
    for start in range(0, columns, DEEP):
        sides = [wide[:, start + j * DEEP : start + (j + 1) * DEEP] for j in range(3)]
        near = table[:, start : start + 3 * DEEP]
        tiles += propagate(still, still + 1, rows, near, sides, 0, 0, row_count + extra)
    grid = jnp.concatenate(tiles, axis=1)[:row_count].reshape(row_count, peers, columns // peers).swapaxes(0, 1)
    arrived = lax.all_to_all(grid, "comp", 0, 0, tiled=True)
    arrived = arrived.reshape(NF * ND, columns // peers)
    (results,) = source_term(still, [arrived], [[0]], quad_index, strength, blocks, turned, 1)
    results = results.reshape(peers, row_count, columns // peers)
    back = lax.all_to_all(results, "comp", 0, 0, tiled=True)
    return back.swapaxes(0, 1).reshape(row_count, columns)


def solution(mesh):
    in_specs = (
        P("comp", ("grp", "space")),
        P(),
        P(("grp", "space")),
        P(("grp", "space")),
        P(),
        P(None, ("grp", "space")),
        P(),
        P(),
        P(),
    )
    out_specs = P("comp", ("grp", "space"))
    return jax.shard_map(shards, mesh=mesh, in_specs=in_specs, out_specs=out_specs, check_vma=False)
```
